1024 devices in a mesh: space: 128 (over y, z), sample: 8 (over x, core).
Axes of the slice: x: 4, y: 8, z: 16, core: 2. Of those that a mesh axis runs over, the one named last changes fastest.
Arguments:
- features: bfloat16 [8, 128, 1, 8, 8, 768], P('sample', 'space'), may hold values from -12 to 12
- wall_mask: int32 [8, 128, 1, 8, 64], P('sample', 'space'), may hold values 0 or 1
- block_positions: int32 [8, 128, 1], P('sample'), may hold values from -1 to 3, as said below
- dw_kernel: float32 [5, 5, 5, 96], replicated, may hold values from -0.5 to 0.5
- norm_gain: float32 [96], replicated, may hold values from 0.1 to 1.9
- norm_bias: float32 [96], replicated, may hold values from -3 to 3
- w_in: bfloat16 [96, 384], replicated, may hold values from -0.625 to 0.625
- b_in: float32 [384], replicated, may hold values from -3 to 3
- w_out: bfloat16 [384, 96], replicated, may hold values from -0.3125 to 0.3125
- b_out: float32 [96], replicated, may hold values from -3 to 3
- layer_scale: float32 [96], replicated, may hold values from 0.3 to 1.5
- upstream: bfloat16 [8, 128, 1, 8, 8, 768], P('sample', 'space'), may hold values from -6 to 6
Outputs:
- mixed: bfloat16 [8, 128, 1, 8, 8, 768], P('sample', 'space')
- grad_features: bfloat16 [8, 128, 1, 8, 8, 768], P('sample', 'space')
- grad_kernel: float32 [5, 5, 5, 96], replicated
- grad_w_in: float32 [96, 384], replicated
- grad_w_out: float32 [384, 96], replicated
- grad_b_in: float32 [384], replicated
- grad_vectors: float32 [4, 96], replicated
The draws below stay inside these ranges and needn't reach their ends.
Inputs may be any that keep to these rules, and one draw needn't show every extreme that they name: `block_positions`: in each layer the live slots come first and hold distinct positions; each layer holds exactly 1 block, in slot 0; the first layer of every sample is full and holds position 3.
All inputs are finite; a program needn't handle non-finite values. No bound on the sum of `wall_mask` on one device may be relied on, other than what follows from the above.
Results may differ from the reference program's by a relative error of at most 0.007.
Values may be sent and summed in bfloat16 or wider, within the bound.
A program may use at most 32 MiB of HBM per device.

```python
import math
import jax
import jax.numpy as jnp
from jax import lax

C = 96
HID = 384
BLOCK = 8
KS = 5
SLOTS = 1
GRID = 2
LAYERS = 128
SAMPLES = 8
VOXELS = 524288


def draw_features(key, part):
    key = jax.random.fold_in(key, 11)
    key_values, key_voxel, key_channel = jax.random.split(key, 3)
    full_shape = (SAMPLES, LAYERS, SLOTS, BLOCK, BLOCK, BLOCK, C)
    voxel_shape = (SAMPLES, LAYERS, SLOTS, BLOCK, BLOCK, BLOCK, 1)
    values = jax.random.normal(key_values, full_shape, jnp.float32)
    voxel_scale = jnp.exp(jax.random.uniform(key_voxel, voxel_shape, jnp.float32, math.log(0.3), math.log(3.0)))
    channel_scale = jnp.exp(jax.random.uniform(key_channel, (C,), jnp.float32, math.log(0.5), math.log(2.0)))
    field = jnp.clip(values * voxel_scale * channel_scale, -12.0, 12.0)
    return field.reshape(SAMPLES, LAYERS, SLOTS, BLOCK, BLOCK, BLOCK * C).astype(jnp.bfloat16)


def draw_block_positions(key, part):
    key = jax.random.fold_in(key, 23)
    key_order, key_count = jax.random.split(key)
    cell_count = GRID * GRID
    scores = jax.random.randint(key_order, (SAMPLES, LAYERS, cell_count), 0, 1 << 20) * cell_count + jnp.arange(cell_count, dtype=jnp.int32)
    first_layer = jnp.arange(LAYERS, dtype=jnp.int32)[None, :, None] == 0
    last_cell = jnp.arange(cell_count, dtype=jnp.int32)[None, None, :] == cell_count - 1
    scores = jnp.where(first_layer & last_cell, -1, scores)
    cell_order = jnp.argsort(scores, axis=-1, stable=True)[..., :SLOTS].astype(jnp.int32)
    counts = jax.random.randint(key_count, (SAMPLES, LAYERS, 1), 1, SLOTS + 1)
    counts = jnp.where(first_layer, SLOTS, counts)
    slot_ids = jnp.arange(SLOTS, dtype=jnp.int32)[None, None, :]
    return jnp.where(slot_ids < counts, cell_order, -1).astype(jnp.int32)


def plant(result, rng, low, top_value):
    longest = result.shape.index(max(result.shape))
    spots = []
    for shift in (0, 1):
        where = [jax.random.randint(jax.random.fold_in(rng, axis), (), 0, length) for axis, length in enumerate(result.shape)]
        where[longest] = (where[longest] + shift) % result.shape[longest]
        spots.append(tuple(where))
    return result.at[spots[0]].set(low).at[spots[1]].set(top_value)


def levels(stream_key, dims, shards, least, top_value):
    level = 1.0
    for dim, shards_of in shards:
        heights = jax.random.uniform(jax.random.fold_in(jax.random.fold_in(stream_key, 6), dim), (shards_of,), jnp.float32, least / len(shards), top_value / len(shards))
        level = level * jnp.repeat(jnp.exp(heights), dims[dim] // shards_of).reshape((-1,) + (1,) * (len(dims) - 1 - dim))
    return level


def scatter_about(rng, extent, deviation, bound, shards=(), held_as=jnp.bfloat16):
    result = deviation * jax.random.normal(rng, extent, jnp.float32)
    if shards:
        result = result * levels(rng, extent, shards, -0.22, 0.18)
    return jnp.clip(result, -bound, bound).astype(held_as)


def setup_inputs(seed: int = 0) -> dict:
    streams_of = jax.random.split(jax.random.key(seed), 13)
    return {
        "features": draw_features(jax.random.fold_in(streams_of[12], 71), 0),
        "wall_mask": plant((jax.random.randint(streams_of[1], (SAMPLES, LAYERS, SLOTS, BLOCK, BLOCK * BLOCK), 0, 4) < 1).astype(jnp.int32), jax.random.fold_in(streams_of[1], 1), 0, 1),
        "block_positions": draw_block_positions(jax.random.fold_in(streams_of[12], 71), 0),
        "dw_kernel": scatter_about(streams_of[3], (KS, KS, KS, C), (KS * KS * KS) ** -0.5, 0.5, (), jnp.float32),
        "norm_gain": jnp.clip(1.0 + 0.18 * jax.random.normal(streams_of[4], (C,), jnp.float32), 0.1, 1.9),
        "norm_bias": scatter_about(streams_of[5], (C,), 0.5, 3.0, (), jnp.float32),
        "w_in": scatter_about(streams_of[6], (C, HID), C ** -0.5, 0.625),
        "b_in": scatter_about(streams_of[7], (HID,), 0.5, 3.0, (), jnp.float32),
        "w_out": scatter_about(streams_of[8], (HID, C), HID ** -0.5, 0.3125),
        "b_out": scatter_about(streams_of[9], (C,), 0.5, 3.0, (), jnp.float32),
        "layer_scale": jnp.clip(jnp.exp(jax.random.uniform(streams_of[10], (C,), jnp.float32, math.log(0.3), math.log(1.5))), 0.3, 1.5),
        "upstream": scatter_about(streams_of[11], (SAMPLES, LAYERS, SLOTS, BLOCK, BLOCK, BLOCK * C), 1.0, 6.0, ((0, 8), (1, 128))),
    }


GELU_SCALE = 0.7978845608028654
GELU_CUBIC = 0.044715
NORM_EPS = 1e-06

def gelu_value(pre_act):
    inner = GELU_SCALE * (pre_act + GELU_CUBIC * pre_act * pre_act * pre_act)
    return 0.5 * pre_act * (1.0 + jnp.tanh(inner))

def gelu_slope(pre_act):
    inner = GELU_SCALE * (pre_act + GELU_CUBIC * pre_act * pre_act * pre_act)
    tanh_value = jnp.tanh(inner)
    return 0.5 * (1.0 + tanh_value) + 0.5 * pre_act * (1.0 - tanh_value * tanh_value) * GELU_SCALE * (1.0 + 3.0 * GELU_CUBIC * pre_act * pre_act)

def expand_fluid(wall_rows, channels):
    block_edge = wall_rows.shape[-2]
    lead_shape = wall_rows.shape[:-2]
    fluid_mask = (1 - wall_rows).astype(jnp.bfloat16).reshape(lead_shape + (block_edge, block_edge, block_edge, 1))
    fluid_mask = jnp.broadcast_to(fluid_mask, lead_shape + (block_edge, block_edge, block_edge, channels))
    return fluid_mask.reshape(lead_shape + (block_edge, block_edge, block_edge * channels))

def edge_range(step_now, block_edge):
    if step_now < 0:
        return (block_edge - 2, block_edge)
    if step_now > 0:
        return (0, 2)
    return (0, block_edge)

def select_blocks(source, own_pos, source_pos, step_y, step_x, grid_side):
    own_y = own_pos // grid_side
    own_x = own_pos % grid_side
    target_y = own_y + step_y
    target_x = own_x + step_x
    inside = (own_pos >= 0) & (target_y >= 0) & (target_y < grid_side) & (target_x >= 0) & (target_x < grid_side)
    target = target_y * grid_side + target_x
    match = (source_pos[None, :] == target[:, None]) & inside[:, None] & (source_pos[None, :] >= 0)
    chosen = jnp.where(match[:, :, None, None, None], source[None], jnp.zeros((), source.dtype))
    return lax.optimization_barrier(jnp.sum(chosen, axis=1)).astype(source.dtype)

def assemble(own_field, below_rims, above_rims, own_pos, below_pos, above_pos, grid_side):
    block_edge = own_field.shape[1]
    channels = own_field.shape[3] // block_edge
    row_parts = []
    for step_y in (-1, 0, 1):
        col_parts = []
        for step_x in (-1, 0, 1):
            y_low, y_high = edge_range(step_y, block_edge)
            x_low, x_high = edge_range(step_x, block_edge)
            pieces = []
            for source, source_pos in ((below_rims, below_pos), (own_field, own_pos), (above_rims, above_pos)):
                trimmed = source[:, :, y_low:y_high, x_low * channels:x_high * channels]
                pieces.append(select_blocks(trimmed, own_pos, source_pos, step_y, step_x, grid_side))
            col_parts.append(jnp.concatenate(pieces, axis=1))
        row_parts.append(jnp.concatenate(col_parts, axis=3))
    return jnp.concatenate(row_parts, axis=2)

def depthwise(padded, dw_kernel, block_edge):
    channels = dw_kernel.shape[3]
    tap_count = dw_kernel.shape[0]
    running = jnp.zeros((padded.shape[0], block_edge, block_edge, block_edge * channels), jnp.float32)
    for tap_z in range(tap_count):
        for tap_y in range(tap_count):
            for tap_x in range(tap_count):
                weight_row = jnp.tile(dw_kernel[tap_z, tap_y, tap_x], block_edge)
                window = padded[:, tap_z:tap_z + block_edge, tap_y:tap_y + block_edge, tap_x * channels:(tap_x + block_edge) * channels]
                running = running + window.astype(jnp.float32) * weight_row
    return running

def kernel_grad(padded, grad_conv, block_edge, tap_count):
    channels = padded.shape[3] // (block_edge + tap_count - 1)
    grad_wide = grad_conv.astype(jnp.float32)
    rows_list = []
    for tap_z in range(tap_count):
        for tap_y in range(tap_count):
            for tap_x in range(tap_count):
                window = padded[:, tap_z:tap_z + block_edge, tap_y:tap_y + block_edge, tap_x * channels:(tap_x + block_edge) * channels]
                per_lane = lax.optimization_barrier(jnp.sum(window.astype(jnp.float32) * grad_wide, axis=(0, 1, 2)))
                rows_list.append(lax.optimization_barrier(jnp.sum(per_lane.reshape(block_edge, channels), axis=0)))
    return jnp.stack(rows_list).reshape(tap_count, tap_count, tap_count, channels)

def dense_step(conv_slot, field_slot, live_value, upstream_slot, norm_gain, norm_bias, w_in, b_in, w_out, b_out, layer_scale):
    channels = norm_gain.shape[0]
    slot_shape = field_slot.shape
    conv_rows = conv_slot.reshape(-1, channels)
    row_mean = lax.optimization_barrier(jnp.mean(conv_rows, axis=1, keepdims=True))
    centred = conv_rows - row_mean
    row_var = lax.optimization_barrier(jnp.mean(centred * centred, axis=1, keepdims=True))
    inv_std = lax.rsqrt(row_var + NORM_EPS)
    unit_rows = centred * inv_std
    normed = (unit_rows * norm_gain + norm_bias).astype(jnp.bfloat16)
    pre_act = jnp.dot(normed, w_in, preferred_element_type=jnp.float32) + b_in
    activated = gelu_value(pre_act).astype(jnp.bfloat16)
    branch = jnp.dot(activated, w_out, preferred_element_type=jnp.float32) + b_out
    field_rows = field_slot.reshape(-1, channels).astype(jnp.float32)
    mixed = ((field_rows + layer_scale * branch) * live_value).astype(jnp.bfloat16)
    seed_grad = upstream_slot.reshape(-1, channels).astype(jnp.float32) * live_value
    scale_grad = lax.optimization_barrier(jnp.sum(seed_grad * branch, axis=0))
    grad_branch = (seed_grad * layer_scale).astype(jnp.bfloat16)
    bout_grad = lax.optimization_barrier(jnp.sum(grad_branch.astype(jnp.float32), axis=0))
    wout_grad = jnp.dot(activated.T, grad_branch, preferred_element_type=jnp.float32)
    grad_act = jnp.dot(grad_branch, w_out.T, preferred_element_type=jnp.float32)
    grad_pre = (grad_act * gelu_slope(pre_act)).astype(jnp.bfloat16)
    bin_grad = lax.optimization_barrier(jnp.sum(grad_pre.astype(jnp.float32), axis=0))
    win_grad = jnp.dot(normed.T, grad_pre, preferred_element_type=jnp.float32)
    grad_normed = jnp.dot(grad_pre, w_in.T, preferred_element_type=jnp.float32)
    gain_grad = lax.optimization_barrier(jnp.sum(grad_normed * unit_rows, axis=0))
    bias_grad = lax.optimization_barrier(jnp.sum(grad_normed, axis=0))
    scaled = grad_normed * norm_gain
    grad_conv = inv_std * (scaled - lax.optimization_barrier(jnp.mean(scaled, axis=1, keepdims=True)) - unit_rows * lax.optimization_barrier(jnp.mean(scaled * unit_rows, axis=1, keepdims=True)))
    grad_conv = grad_conv.astype(jnp.bfloat16).reshape(slot_shape)
    vectors = jnp.stack([gain_grad, bias_grad, bout_grad, scale_grad])
    return (mixed.reshape(slot_shape), grad_conv, (win_grad, wout_grad, bin_grad, vectors))

def neighbours(field, positions, block_edge):
    rims_below = jnp.concatenate([jnp.zeros_like(field[:1, :, block_edge - 2:]), field[:-1, :, block_edge - 2:]], axis=0)
    rims_above = jnp.concatenate([field[1:, :, :2], jnp.zeros_like(field[:1, :, :2])], axis=0)
    empty_row = jnp.full(positions[:1].shape, -1, jnp.int32)
    below_pos = jnp.concatenate([empty_row, positions[:-1]], axis=0)
    above_pos = jnp.concatenate([positions[1:], empty_row], axis=0)
    return (rims_below, rims_above, below_pos, above_pos)

def reference(features, wall_mask, block_positions, dw_kernel, norm_gain, norm_bias, w_in, b_in, w_out, b_out, layer_scale, upstream):
    channels = dw_kernel.shape[3]
    tap_count = dw_kernel.shape[0]
    block_edge = features.shape[3]
    hidden_units = w_in.shape[1]
    flipped = dw_kernel[::-1, ::-1, ::-1]
    start = (jnp.zeros(dw_kernel.shape, jnp.float32), jnp.zeros(w_in.shape, jnp.float32), jnp.zeros(w_out.shape, jnp.float32), jnp.zeros((hidden_units,), jnp.float32), jnp.zeros((4, channels), jnp.float32))

    def slot_step(slot_items):
        return dense_step(slot_items[0], slot_items[1], slot_items[2], slot_items[3], norm_gain, norm_bias, w_in, b_in, w_out, b_out, layer_scale)

    def one_sample(sums, sample_items):
        sample_field, sample_walls, positions, sample_up = sample_items
        live_flag = (positions >= 0).astype(jnp.bfloat16)
        fluid_mask = expand_fluid(sample_walls, channels)
        masked = sample_field * fluid_mask * live_flag[:, :, None, None, None]
        rims_below, rims_above, below_pos, above_pos = neighbours(masked, positions, block_edge)

        def first_pass(carried, layer_items):
            own_field, below_rims, above_rims, own_pos, low_pos, high_pos, field_layer, up_layer, live_layer = layer_items
            padded = assemble(own_field, below_rims, above_rims, own_pos, low_pos, high_pos, GRID)
            conv_out = depthwise(padded, dw_kernel, block_edge)
            mixed_layer, grad_conv, grads = lax.map(slot_step, (conv_out, field_layer, live_layer.astype(jnp.float32), up_layer))
            kernel_term = kernel_grad(padded, grad_conv, block_edge, tap_count)
            carried = (carried[0] + kernel_term, carried[1] + lax.optimization_barrier(jnp.sum(grads[0], axis=0)), carried[2] + lax.optimization_barrier(jnp.sum(grads[1], axis=0)), carried[3] + lax.optimization_barrier(jnp.sum(grads[2], axis=0)), carried[4] + lax.optimization_barrier(jnp.sum(grads[3], axis=0)))
            return (carried, (mixed_layer, grad_conv))
        sums, (mixed_sample, grad_conv_all) = lax.scan(first_pass, sums, (masked, rims_below, rims_above, positions, below_pos, above_pos, sample_field, sample_up, live_flag))
        grad_below, grad_above, below_again, above_again = neighbours(grad_conv_all, positions, block_edge)

        def second_pass(unused, layer_items):
            own_grad, below_grad, above_grad, own_pos, low_pos, high_pos, fluid_layer, up_layer, live_layer = layer_items
            grad_padded = assemble(own_grad, below_grad, above_grad, own_pos, low_pos, high_pos, GRID)
            back_conv = depthwise(grad_padded, flipped, block_edge)
            live_wide = live_layer.astype(jnp.float32)[:, None, None, None]
            seed_grad = up_layer.astype(jnp.float32) * live_wide
            return (unused, (seed_grad + back_conv * fluid_layer * live_wide).astype(jnp.bfloat16))
        unused_out, grad_sample = lax.scan(second_pass, jnp.zeros((), jnp.float32), (grad_conv_all, grad_below, grad_above, positions, below_again, above_again, fluid_mask, sample_up, live_flag))
        return (sums, (mixed_sample, grad_sample))
    sums, (mixed, grad_features) = lax.scan(one_sample, start, (features, wall_mask, block_positions, upstream))
    factor = 1.0 / math.sqrt(VOXELS)
    return (mixed, grad_features, sums[0] * factor, sums[1] * factor, sums[2] * factor, sums[3] * factor, sums[4] * factor)
```

```python
import math

import jax
import jax.numpy as jnp
from jax import lax
from jax.experimental import pallas as pl
from jax.experimental.pallas import tpu as pltpu
from jax.sharding import PartitionSpec as P

F32 = jnp.float32
BF16 = jnp.bfloat16
MESH = pl.DeviceIdType.MESH

GELU_SCALE = 0.7978845608028654
GELU_CUBIC = 0.044715
NORM_EPS = 1e-06

E = 8
K = 5
C = 96
H = 384
NZ = 16
NY = 8
NS = 8
ROWS = 2
TILE = 16
LANES = 128
W_TILES = 40
K_TILES = 8
W_SHARE = W_TILES // NS
K_SHARE = K_TILES // NS
SHARE = W_SHARE + K_SHARE
PART = -(-SHARE // NY)


def wait_bytes(ref, sem):
    pltpu.make_async_copy(ref, ref, sem).wait()


def send(src, dst, send_sem, recv_sem, device):
    pltpu.make_async_remote_copy(
        src_ref=src,
        dst_ref=dst,
        send_sem=send_sem,
        recv_sem=recv_sem,
        device_id=device,
        device_id_type=MESH,
    ).start()


def send_all(count, me, device, src, dst, send_sem, recv_sem):
    for step in range(1, count):
        peer = lax.rem(me + step, count)
        send(src(peer), dst(step), send_sem, recv_sem, device(peer))


def axis_region(index):
    return jnp.where(index < 2, -1, jnp.where(index < 2 + E, 0, 1))


def shifted(block, tap):
    return pltpu.roll(block, (2 - tap) % E, 1)


def spread_own(dest, column, block, y_index):
    for tap in range(K):
        keep = (axis_region(y_index + tap) == 0).astype(F32)
        dest[tap, column + 2, 2 : 2 + E] = shifted(block, tap) * keep


def clear_sides(dest):
    zeros = jnp.zeros((K, 2, E, E, C), F32)
    dest[:, 0:2, 2 : 2 + E] = zeros
    dest[:, 2 + E : 4 + E, 2 : 2 + E] = zeros


def spread_halo(dest, halo, low, step_y, step_x, exists, y_index):
    for tap in range(K):
        keep_y = (axis_region(y_index + tap) == step_y) & exists
        for region in (-1, 0, 1):
            keep = (keep_y & (step_x == region)).astype(F32)
            first, count = {-1: (0, 2), 0: (2, E), 1: (2 + E, 2)}[region]
            source = (first + E - 2) % E
            block = halo[source : source + count].astype(F32).reshape(count * 2, E, C)
            block = shifted(block, tap).reshape(count, 2, E, C) * keep
            dest[tap, first : first + count, low : low + 2] = block


def conv_planes(field, weights, out, first, last, reverse):
    def plane(index, carry):
        z = lax.rem(index, E)
        total = jnp.zeros((E, E, C), F32)
        for tap_z in range(K):
            for tap_y in range(K):
                window = field[tap_y, :, z + tap_z]
                pair = tap_z * K + tap_y
                for tap_x in range(K):
                    row = weights[K * K - 1 - pair, K - 1 - tap_x] if reverse else weights[pair, tap_x]
                    total = total + window[tap_x : tap_x + E] * row
        out[:, z] = total
        return carry

    lax.fori_loop(first, last, plane, 0)


def body(
    field_ref, wall_ref, pos_ref, dw_ref, gain_ref, bias_ref, win_ref, bin_ref, wout_ref, bout_ref,
    scale_ref, up_ref,
    mixed_ref, gfield_ref, gkernel_ref, gwin_ref, gwout_ref, gbin_ref, gvec_ref,
    weights, padded, gpadded, conv, grad, fluid, field, upstream, mixed,
    normed_all, act_all, gpre_all, gbranch_all, vec_sum, bin_sum, kernel_rows, vec_tile,
    rims, halos, grims, ghalos,
    w_out1, k_out1, w_in1, k_in1, out2, in2, out3, in3, gather4, gather5,
    halo_send, halo_recv, send_sem, recv_sem,
):
    space = lax.axis_index("space")
    sample = lax.axis_index("sample")
    layers = NY * NZ
    chip_y = space // NZ
    chip_z = lax.rem(space, NZ)
    above = (lax.rem(space + 1, layers), sample)
    below = (lax.rem(space + layers - 1, layers), sample)

    def in_sample(peer):
        return (space, peer)

    def in_y(peer):
        return (peer * NZ + chip_z, sample)

    def in_z(peer):
        return (chip_y * NZ + peer, sample)

    barrier = pltpu.get_barrier_semaphore()
    for device in (above, below):
        pl.semaphore_signal(barrier, inc=1, device_id=device, device_id_type=MESH)
    for count, me, device in ((NS, sample, in_sample), (NY, chip_y, in_y), (NZ, chip_z, in_z)):
        for step in range(1, count):
            peer = lax.rem(me + step, count)
            pl.semaphore_signal(barrier, inc=1, device_id=device(peer), device_id_type=MESH)

    y_index = lax.broadcasted_iota(jnp.int32, (E, C), 0)
    lane = lax.broadcasted_iota(jnp.int32, (E, E, E * E), 2)
    sub = lax.broadcasted_iota(jnp.int32, (E, E, E * E), 1)
    walls = jnp.broadcast_to(wall_ref[...].astype(F32)[:, None, :], (E, E, E * E))
    walls = jnp.where(lane // E == sub, walls, 0.0).reshape(E * E, E * E).astype(BF16)
    voxel = lax.broadcasted_iota(jnp.int32, (E * E, C), 0)
    wide = field_ref[...].astype(F32)
    for x in range(E):
        pick = (lax.rem(voxel, E) == x).astype(BF16)
        open_x = 1.0 - jnp.dot(walls, pick, preferred_element_type=F32)
        fluid[x] = open_x.reshape(E, E, C)
        column = wide[:, :, x * C : (x + 1) * C]
        field[x] = column
        masked = column * fluid[x]
        conv[x] = masked
        rims[0, x] = masked[E - 2 :].reshape(2 * E, C).astype(BF16)
        rims[1, x] = masked[:2].reshape(2 * E, C).astype(BF16)

    pl.semaphore_wait(barrier, 2 + NS + NY + NZ - 3)
    send(rims.at[0], halos.at[0], halo_send.at[0], halo_recv.at[0], above)
    send(rims.at[1], halos.at[1], halo_send.at[1], halo_recv.at[1], below)

    wide = up_ref[...].astype(F32)
    for x in range(E):
        upstream[x] = wide[:, :, x * C : (x + 1) * C]
    clear_sides(padded)
    clear_sides(gpadded)

    def own_column(x, carry):
        spread_own(padded, x, conv[x], y_index)
        return carry

    lax.fori_loop(0, E, own_column, 0)

    def spread_weights(pair, carry):
        rows = dw_ref[pair // K, lax.rem(pair, K)]
        weights[pair] = jnp.broadcast_to(rows[:, None, :], (K, E, C))
        return carry

    lax.fori_loop(0, K * K, spread_weights, 0)
    conv_planes(padded, weights, conv, 2, 6, False)

    layer_index = lax.broadcasted_iota(jnp.int32, (1, layers), 1)

    def position(layer):
        return jnp.sum(jnp.where(layer_index == layer, pos_ref[...], 0), axis=1, keepdims=True)

    own_pos, low_pos, high_pos = position(space), position(space - 1), position(space + 1)
    step_low = (low_pos // 2 - own_pos // 2, low_pos % 2 - own_pos % 2)
    step_high = (high_pos // 2 - own_pos // 2, high_pos % 2 - own_pos % 2)

    def place_halos(dest, received):
        spread_halo(dest, received.at[0], 0, *step_low, space > 0, y_index)
        spread_halo(dest, received.at[1], 2 + E, *step_high, space < layers - 1, y_index)

    for side in range(2):
        wait_bytes(halos.at[side], halo_recv.at[side])
    place_halos(padded, halos)
    conv_planes(padded, weights, conv, 6, 10, False)

    vec_sum[...] = jnp.zeros_like(vec_sum)
    bin_sum[...] = jnp.zeros_like(bin_sum)
    gain, bias, bout, scale = gain_ref[...], bias_ref[...], bout_ref[...], scale_ref[...]
    count = ROWS * E * E

    def by_sublane(values):
        return jnp.sum(values.reshape(count // E, E, values.shape[1]), axis=0)

    def dense(step, carry):
        columns = pl.ds(step * ROWS, ROWS)
        rows = pl.ds(pl.multiple_of(step * count, count), count)
        conv_rows = conv[columns].reshape(count, C)
        row_mean = jnp.mean(conv_rows, axis=1, keepdims=True)
        centred = conv_rows - row_mean
        row_var = jnp.mean(centred * centred, axis=1, keepdims=True)
        inv_std = lax.rsqrt(row_var + NORM_EPS)
        unit_rows = centred * inv_std
        normed = (unit_rows * gain + bias).astype(BF16)
        pre_act = jnp.dot(normed, win_ref[...], preferred_element_type=F32) + bin_ref[...]
        square = pre_act * pre_act
        tanh_value = jnp.tanh(GELU_SCALE * (pre_act + GELU_CUBIC * square * pre_act))
        half = 0.5 * (1.0 + tanh_value)
        activated = (pre_act * half).astype(BF16)
        slope = half + 0.5 * pre_act * (1.0 - tanh_value * tanh_value) * (
            GELU_SCALE * (1.0 + 3.0 * GELU_CUBIC * square)
        )
        branch = (
            lax.dot_general(
                activated, wout_ref[...], (((1,), (1,)), ((), ())), preferred_element_type=F32
            )
            + bout
        )
        mixed[columns] = (field[columns].reshape(count, C) + scale * branch).reshape(ROWS, E, E, C)
        seed = upstream[columns].reshape(count, C)
        grad_branch = (seed * scale).astype(BF16)
        grad_act = jnp.dot(grad_branch, wout_ref[...], preferred_element_type=F32)
        grad_pre = (grad_act * slope).astype(BF16)
        grad_normed = lax.dot_general(
            grad_pre, win_ref[...], (((1,), (1,)), ((), ())), preferred_element_type=F32
        )
        scaled = grad_normed * gain
        grad_conv = inv_std * (
            scaled
            - jnp.mean(scaled, axis=1, keepdims=True)
            - unit_rows * jnp.mean(scaled * unit_rows, axis=1, keepdims=True)
        )
        grad[columns] = grad_conv.astype(BF16).astype(F32).reshape(ROWS, E, E, C)
        normed_all[rows] = normed
        act_all[rows] = activated
        gpre_all[rows] = grad_pre
        gbranch_all[rows] = grad_branch
        vec_sum[0] += by_sublane(grad_normed * unit_rows)
        vec_sum[1] += by_sublane(grad_normed)
        vec_sum[2] += by_sublane(grad_branch.astype(F32))
        vec_sum[3] += by_sublane(seed * branch)
        bin_sum[...] += by_sublane(grad_pre.astype(F32))
        return carry

    lax.fori_loop(0, E // ROWS, dense, 0)

    def grad_rims(x, carry):
        grims[0, x] = grad[x, E - 2 :].reshape(2 * E, C).astype(BF16)
        grims[1, x] = grad[x, :2].reshape(2 * E, C).astype(BF16)
        return carry

    lax.fori_loop(0, E, grad_rims, 0)
    send(grims.at[0], ghalos.at[0], halo_send.at[2], halo_recv.at[2], above)
    send(grims.at[1], ghalos.at[1], halo_send.at[3], halo_recv.at[3], below)

    by_rows = (((0,), (0,)), ((), ()))
    for base, left, right in ((0, normed_all, gpre_all), (18, gbranch_all, act_all)):
        product = lax.dot_general(left[...], right[...], by_rows, preferred_element_type=F32)
        for part in range(H // LANES):
            piece = product[:, part * LANES : (part + 1) * LANES].astype(BF16)
            w_out1[base + 6 * part : base + 6 * part + 6] = piece.reshape(6, TILE, LANES)
    vec_tile[...] = jnp.zeros_like(vec_tile)
    bin_row = jnp.sum(bin_sum[...], axis=0, keepdims=True)
    for part in range(H // LANES):
        vec_tile[part : part + 1] = bin_row[:, part * LANES : (part + 1) * LANES]
    for row in range(4):
        vec_tile[3 + row : 4 + row, 0:C] = jnp.sum(vec_sum[row], axis=0, keepdims=True)
    w_out1[36] = vec_tile[...].astype(BF16)
    w_out1[37:W_TILES] = jnp.zeros((W_TILES - 37, TILE, LANES), BF16)
    send_all(
        NS, sample, in_sample, lambda peer: w_out1.at[pl.ds(peer * W_SHARE, W_SHARE)],
        lambda step: w_in1.at[step - 1], send_sem.at[0], recv_sem.at[0],
    )

    kernel_rows[...] = jnp.zeros_like(kernel_rows)

    def kernel_pair(pair, carry):
        tap_z = pair // K
        tap_y = lax.rem(pair, K)
        sums = [jnp.zeros((E, C), F32) for _ in range(K)]
        for z in range(E):
            window = padded[tap_y, :, z + tap_z]
            factor = grad[:, z]
            for tap_x in range(K):
                sums[tap_x] = sums[tap_x] + jnp.sum(window[tap_x : tap_x + E] * factor, axis=0)
        for tap_x in range(K):
            total = jnp.sum(sums[tap_x], axis=0, keepdims=True)
            kernel_rows[pl.ds(pair * K + tap_x, 1), 0:C] = total
        return carry

    lax.fori_loop(0, K * K, kernel_pair, 0)
    k_out1[...] = kernel_rows[...].astype(BF16).reshape(K_TILES, TILE, LANES)
    send_all(
        NS, sample, in_sample, lambda peer: k_out1.at[pl.ds(peer * K_SHARE, K_SHARE)],
        lambda step: k_in1.at[step - 1], send_sem.at[1], recv_sem.at[1],
    )

    def own_grad_column(x, carry):
        spread_own(gpadded, x, grad[x], y_index)
        return carry

    lax.fori_loop(0, E, own_grad_column, 0)
    conv_planes(gpadded, weights, conv, 2, 6, True)

    wait_bytes(w_in1, recv_sem.at[0])
    wait_bytes(k_in1, recv_sem.at[1])
    w_total = w_out1[pl.ds(sample * W_SHARE, W_SHARE)].astype(F32)
    k_total = k_out1[pl.ds(sample * K_SHARE, K_SHARE)].astype(F32)
    for step in range(NS - 1):
        w_total = w_total + w_in1[step].astype(F32)
        k_total = k_total + k_in1[step].astype(F32)
    out2[0:W_SHARE] = w_total.astype(BF16)
    out2[W_SHARE:SHARE] = k_total.astype(BF16)
    if NY * PART > SHARE:
        out2[SHARE : NY * PART] = jnp.zeros((NY * PART - SHARE, TILE, LANES), BF16)
    send_all(
        NY, chip_y, in_y, lambda peer: out2.at[pl.ds(peer * PART, PART)],
        lambda step: in2.at[step - 1], send_sem.at[2], recv_sem.at[2],
    )

    for side in range(2):
        wait_bytes(ghalos.at[side], halo_recv.at[2 + side])
    place_halos(gpadded, ghalos)
    conv_planes(gpadded, weights, conv, 6, 10, True)

    wait_bytes(in2, recv_sem.at[2])
    total = out2[pl.ds(chip_y * PART, PART)].astype(F32)
    for step in range(NY - 1):
        total = total + in2[step].astype(F32)
    out3[...] = total.astype(BF16)
    send_all(
        NZ, chip_z, in_z, lambda peer: out3,
        lambda step: in3.at[step - 1], send_sem.at[3], recv_sem.at[3],
    )

    for x in range(E):
        lanes = slice(x * C, (x + 1) * C)
        mixed_ref[:, :, lanes] = mixed[x].astype(BF16)
        gfield_ref[:, :, lanes] = (upstream[x] + conv[x] * fluid[x]).astype(BF16)

    wait_bytes(in3, recv_sem.at[3])
    total = out3[...].astype(F32)
    for step in range(NZ - 1):
        total = total + in3[step].astype(F32)
    mine = pl.ds(chip_y * PART, PART)
    gather4[mine] = total.astype(BF16)
    send_all(
        NY, chip_y, in_y, lambda peer: gather4.at[mine],
        lambda step: gather4.at[mine], send_sem.at[4], recv_sem.at[4],
    )
    wait_bytes(gather4.at[0 : (NY - 1) * PART], recv_sem.at[4])
    gather5[sample] = gather4[0:SHARE]
    send_all(
        NS, sample, in_sample, lambda peer: gather5.at[sample],
        lambda step: gather5.at[sample], send_sem.at[5], recv_sem.at[5],
    )
    wait_bytes(gather5.at[0 : NS - 1], recv_sem.at[5])

    factor = 1.0 / math.sqrt(NS * layers * E**3)

    def tile_of(index):
        return gather5[index // W_SHARE, index % W_SHARE].astype(F32) * factor

    for part in range(H // LANES):
        lanes = slice(part * LANES, (part + 1) * LANES)
        for row in range(6):
            gwin_ref[row * TILE : (row + 1) * TILE, lanes] = tile_of(6 * part + row)
            gwout_ref[row * TILE : (row + 1) * TILE, lanes] = tile_of(18 + 6 * part + row)
    last = tile_of(36)
    for part in range(H // LANES):
        gbin_ref[0:1, part * LANES : (part + 1) * LANES] = last[part : part + 1]
    gvec_ref[...] = last[3:7, 0:C]
    rows = gather5[:, W_SHARE:SHARE].astype(F32).reshape(K_TILES * TILE, LANES)[:, 0:C] * factor
    for pair in range(K * K):
        gkernel_ref[pair // K, pair % K] = rows[pair * K : (pair + 1) * K]

    for side in range(2):
        wait_bytes(rims.at[side], halo_send.at[side])
        wait_bytes(grims.at[side], halo_send.at[2 + side])
    for index, ref in enumerate((w_in1, k_in1, in2, in3, gather4.at[0 : (NY - 1) * PART], gather5.at[0 : NS - 1])):
        wait_bytes(ref, send_sem.at[index])


def local(
    features, wall_mask, block_positions, dw_kernel, norm_gain, norm_bias, w_in, b_in, w_out, b_out,
    layer_scale, upstream,
):
    voxels = (E, E, E, C)
    spread = (K, E + 4, E + 4, E, C)
    rows = E**3
    vmem = pl.BlockSpec(memory_space=pltpu.VMEM)
    outs = (
        jax.ShapeDtypeStruct((E, E, E * C), BF16),
        jax.ShapeDtypeStruct((E, E, E * C), BF16),
        jax.ShapeDtypeStruct((K, K, K, C), F32),
        jax.ShapeDtypeStruct((C, H), F32),
        jax.ShapeDtypeStruct((C, H), F32),
        jax.ShapeDtypeStruct((1, H), F32),
        jax.ShapeDtypeStruct((4, C), F32),
    )
    scratch = [
        pltpu.VMEM((K * K, K, E, C), F32),
        pltpu.VMEM(spread, F32),
        pltpu.VMEM(spread, F32),
        pltpu.VMEM(voxels, F32),
        pltpu.VMEM(voxels, F32),
        pltpu.VMEM(voxels, F32),
        pltpu.VMEM(voxels, F32),
        pltpu.VMEM(voxels, F32),
        pltpu.VMEM(voxels, F32),
        pltpu.VMEM((rows, C), BF16),
        pltpu.VMEM((rows, H), BF16),
        pltpu.VMEM((rows, H), BF16),
        pltpu.VMEM((rows, C), BF16),
        pltpu.VMEM((4, E, C), F32),
        pltpu.VMEM((E, H), F32),
        pltpu.VMEM((K_TILES * TILE, LANES), F32),
        pltpu.VMEM((TILE, LANES), F32),
        pltpu.VMEM((2, E, 2 * E, C), BF16),
        pltpu.VMEM((2, E, 2 * E, C), BF16),
        pltpu.VMEM((2, E, 2 * E, C), BF16),
        pltpu.VMEM((2, E, 2 * E, C), BF16),
        pltpu.VMEM((W_TILES, TILE, LANES), BF16),
        pltpu.VMEM((K_TILES, TILE, LANES), BF16),
        pltpu.VMEM((NS - 1, W_SHARE, TILE, LANES), BF16),
        pltpu.VMEM((NS - 1, K_SHARE, TILE, LANES), BF16),
        pltpu.VMEM((NY * PART, TILE, LANES), BF16),
        pltpu.VMEM((NY - 1, PART, TILE, LANES), BF16),
        pltpu.VMEM((PART, TILE, LANES), BF16),
        pltpu.VMEM((NZ - 1, PART, TILE, LANES), BF16),
        pltpu.VMEM((NY * PART, TILE, LANES), BF16),
        pltpu.VMEM((NS, SHARE, TILE, LANES), BF16),
        pltpu.SemaphoreType.DMA((4,)),
        pltpu.SemaphoreType.DMA((4,)),
        pltpu.SemaphoreType.DMA((6,)),
        pltpu.SemaphoreType.DMA((6,)),
    ]
    results = pl.pallas_call(
        body,
        out_shape=outs,
        in_specs=[vmem] * 12,
        out_specs=[vmem] * 7,
        scratch_shapes=scratch,
        compiler_params=pltpu.CompilerParams(
            collective_id=0, has_side_effects=True, vmem_limit_bytes=48 * 1024 * 1024
        ),
        cost_estimate=pl.CostEstimate(flops=400_000_000, bytes_accessed=1_500_000, transcendentals=200_000),
        name="block_step",
    )(
        features[0, 0, 0],
        wall_mask[0, 0, 0],
        block_positions[:, :, 0],
        dw_kernel,
        norm_gain[None],
        norm_bias[None],
        w_in,
        b_in[None],
        w_out.T,
        b_out[None],
        layer_scale[None],
        upstream[0, 0, 0],
    )
    mixed, gfield, gkernel, gwin, gwout, gbin, gvec = results
    return (mixed[None, None, None], gfield[None, None, None], gkernel, gwin, gwout.T, gbin[0], gvec)


def solution(mesh):
    sharded = P("sample", "space", None, None, None, None)
    return jax.shard_map(
        local,
        mesh=mesh,
        in_specs=(
            sharded,
            P("sample", "space", None, None, None),
            P("sample", None, None),
            P(), P(), P(), P(), P(), P(), P(), P(),
            sharded,
        ),
        out_specs=(sharded, sharded, P(), P(), P(), P(), P()),
        check_vma=False,
    )
```

```python
import math

import jax
import jax.numpy as jnp
from jax import lax
from jax.experimental import pallas as pl
from jax.experimental.pallas import tpu as pltpu
from jax.sharding import PartitionSpec as P

F32 = jnp.float32
BF16 = jnp.bfloat16
MESH = pl.DeviceIdType.MESH

GELU_SCALE = 0.7978845608028654
GELU_CUBIC = 0.044715
NORM_EPS = 1e-06

VMEM_BYTES = 62 * 1024 * 1024
E = 8
K = 5
C = 96
H = 384
NZ = 16
NY = 8
NS = 8
ROWS = 2
TILE = 16
LANES = 128
W_TILES = 40
K_TILES = 8
W_SHARE = W_TILES // NS
K_SHARE = K_TILES // NS
PART = -(-W_SHARE // NY)


def wait_bytes(ref, sem):
    pltpu.make_async_copy(ref, ref, sem).wait()


def send(src, dst, send_sem, recv_sem, device):
    pltpu.make_async_remote_copy(
        src_ref=src,
        dst_ref=dst,
        send_sem=send_sem,
        recv_sem=recv_sem,
        device_id=device,
        device_id_type=MESH,
    ).start()


def ring_order(count):
    return sorted(range(1, count), key=lambda step: -min(step, count - step))


def sample_order():
    chips = NS // 2
    steps = [(x, core) for x in range(chips) for core in range(2) if (x, core) != (0, 0)]
    return sorted(steps, key=lambda step: -min(step[0], chips - step[0]))


def send_all(peers, src, dst, send_sem, recv_sem):
    for slot, (index, device) in enumerate(peers):
        send(src(index), dst(slot), send_sem, recv_sem, device)


def add_all(total, parts, count):
    total = total.astype(F32)
    for slot in range(count):
        total = total + parts[slot].astype(F32)
    return total


def axis_region(index):
    return jnp.where(index < 2, -1, jnp.where(index < 2 + E, 0, 1))


def shifted(block, tap):
    return pltpu.roll(block, (2 - tap) % E, 1)


def spread_own(dest, column, block, y_index):
    for tap in range(K):
        keep = (axis_region(y_index + tap) == 0).astype(F32)
        dest[tap, column + 2, 2 : 2 + E] = shifted(block, tap) * keep


def clear_sides(dest):
    zeros = jnp.zeros((K, 2, E, E, C), F32)
    dest[:, 0:2, 2 : 2 + E] = zeros
    dest[:, 2 + E : 4 + E, 2 : 2 + E] = zeros


def spread_halo(dest, halo, low, step_y, step_x, exists, y_index):
    for tap in range(K):
        keep_y = (axis_region(y_index + tap) == step_y) & exists
        for region in (-1, 0, 1):
            keep = (keep_y & (step_x == region)).astype(F32)
            first, count = {-1: (0, 2), 0: (2, E), 1: (2 + E, 2)}[region]
            source = (first + E - 2) % E
            block = halo[source : source + count].astype(F32).reshape(count * 2, E, C)
            block = shifted(block, tap).reshape(count, 2, E, C) * keep
            dest[tap, first : first + count, low : low + 2] = block


def conv_planes(field, weights, out, first, last, reverse):
    def plane(index, carry):
        z = lax.rem(index, E)
        total = jnp.zeros((E, E, C), F32)
        for tap_z in range(K):
            for tap_y in range(K):
                window = field[tap_y, :, z + tap_z]
                pair = tap_z * K + tap_y
                for tap_x in range(K):
                    row = weights[K * K - 1 - pair, K - 1 - tap_x] if reverse else weights[pair, tap_x]
                    total = total + window[tap_x : tap_x + E] * row
        out[:, z] = total
        return carry

    lax.fori_loop(first, last, plane, 0)


def body(
    field_hbm, wall_hbm, pos_hbm, dw_hbm, gain_hbm, bias_hbm, win_hbm, bin_hbm, wout_hbm, bout_hbm,
    scale_hbm, up_hbm,
    mixed_hbm, gfield_hbm, gkernel_hbm, gwin_hbm, gwout_hbm, gbin_hbm, gvec_hbm,
    weights, padded, gpadded, conv, grad, fluid, field, upstream, mixed,
    normed_all, act_all, gpre_all, gbranch_all, vec_sum, bin_sum, kernel_rows, vec_tile,
    rims, halos, grims, ghalos,
    w_out1, w_in1, w_out2, w_in2, w_out3, w_in3, w_share, w_all,
    k_out1, k_in1, k_out2, k_in2, k_out3, k_in3, k_all,
    field_ref, wall_ref, pos_ref, dw_ref, gain_ref, bias_ref, win_ref, bin_ref, wout_ref, bout_ref,
    scale_ref, up_ref,
    mixed_ref, gfield_ref, gkernel_ref, gwin_ref, gwout_ref, gbin_ref, gvec_ref,
    halo_send, halo_recv, send_sem, recv_sem, load_sem, store_sem,
):
    stores = [
        pltpu.make_async_copy(source, dest, store_sem.at[index])
        for index, (source, dest) in enumerate((
            (mixed_ref, mixed_hbm), (gfield_ref, gfield_hbm), (gkernel_ref, gkernel_hbm),
            (gwin_ref, gwin_hbm), (gwout_ref, gwout_hbm), (gbin_ref, gbin_hbm), (gvec_ref, gvec_hbm),
        ))
    ]
    loads = [
        pltpu.make_async_copy(source, dest, load_sem.at[index])
        for index, (source, dest) in enumerate((
            (field_hbm, field_ref), (wall_hbm, wall_ref), (dw_hbm, dw_ref), (up_hbm, up_ref),
            (pos_hbm, pos_ref), (gain_hbm, gain_ref), (bias_hbm, bias_ref), (win_hbm, win_ref),
            (bin_hbm, bin_ref), (wout_hbm, wout_ref), (bout_hbm, bout_ref), (scale_hbm, scale_ref),
        ))
    ]
    for load in loads:
        load.start()
    space = lax.axis_index("space")
    sample = lax.axis_index("sample")
    layers = NY * NZ
    chip_y = space // NZ
    chip_z = lax.rem(space, NZ)
    above = (lax.rem(space + 1, layers), sample)
    below = (lax.rem(space + layers - 1, layers), sample)

    x_peers = []
    for step_x, step_core in sample_order():
        x = lax.rem(sample // 2 + step_x, NS // 2)
        index = x * 2 + lax.rem(sample + step_core, 2)
        x_peers.append((index, (space, index)))
    y_peers = []
    for step in ring_order(NY):
        index = lax.rem(chip_y + step, NY)
        y_peers.append((index, (index * NZ + chip_z, sample)))
    z_peers = []
    for step in ring_order(NZ):
        index = lax.rem(chip_z + step, NZ)
        z_peers.append((index, (chip_y * NZ + index, sample)))

    barrier = pltpu.get_barrier_semaphore()
    partners = [above, below] + [device for _, device in x_peers + y_peers + z_peers]
    for device in partners:
        pl.semaphore_signal(barrier, inc=1, device_id=device, device_id_type=MESH)

    loads[0].wait()
    loads[1].wait()
    y_index = lax.broadcasted_iota(jnp.int32, (E, C), 0)
    lane = lax.broadcasted_iota(jnp.int32, (E, E, E * E), 2)
    sub = lax.broadcasted_iota(jnp.int32, (E, E, E * E), 1)
    walls = jnp.broadcast_to(wall_ref[...].astype(F32)[:, None, :], (E, E, E * E))
    walls = jnp.where(lane // E == sub, walls, 0.0).reshape(E * E, E * E).astype(BF16)
    voxel = lax.broadcasted_iota(jnp.int32, (E * E, C), 0)
    wide = field_ref[...].astype(F32)
    for x in range(E):
        pick = (lax.rem(voxel, E) == x).astype(BF16)
        open_x = 1.0 - jnp.dot(walls, pick, preferred_element_type=F32)
        fluid[x] = open_x.reshape(E, E, C)
        column = wide[:, :, x * C : (x + 1) * C]
        field[x] = column
        masked = column * fluid[x]
        conv[x] = masked
        rims[0, x] = masked[E - 2 :].reshape(2 * E, C).astype(BF16)
        rims[1, x] = masked[:2].reshape(2 * E, C).astype(BF16)

    pl.semaphore_wait(barrier, len(partners))
    send(rims.at[0], halos.at[0], halo_send.at[0], halo_recv.at[0], above)
    send(rims.at[1], halos.at[1], halo_send.at[1], halo_recv.at[1], below)

    for load in loads[2:]:
        load.wait()
    wide = up_ref[...].astype(F32)
    for x in range(E):
        upstream[x] = wide[:, :, x * C : (x + 1) * C]
    clear_sides(padded)
    clear_sides(gpadded)

    def own_column(x, carry):
        spread_own(padded, x, conv[x], y_index)
        return carry

    lax.fori_loop(0, E, own_column, 0)

    def spread_weights(pair, carry):
        rows = dw_ref[pair // K, lax.rem(pair, K)]
        weights[pair] = jnp.broadcast_to(rows[:, None, :], (K, E, C))
        return carry

    lax.fori_loop(0, K * K, spread_weights, 0)
    conv_planes(padded, weights, conv, 2, 6, False)

    layer_index = lax.broadcasted_iota(jnp.int32, (1, layers), 1)

    def position(layer):
        return jnp.sum(jnp.where(layer_index == layer, pos_ref[...], 0), axis=1, keepdims=True)

    own_pos, low_pos, high_pos = position(space), position(space - 1), position(space + 1)
    step_low = (low_pos // 2 - own_pos // 2, low_pos % 2 - own_pos % 2)
    step_high = (high_pos // 2 - own_pos // 2, high_pos % 2 - own_pos % 2)

    def place_halos(dest, received):
        spread_halo(dest, received.at[0], 0, *step_low, space > 0, y_index)
        spread_halo(dest, received.at[1], 2 + E, *step_high, space < layers - 1, y_index)

    for side in range(2):
        wait_bytes(halos.at[side], halo_recv.at[side])
    place_halos(padded, halos)
    conv_planes(padded, weights, conv, 6, 10, False)

    vec_sum[...] = jnp.zeros_like(vec_sum)
    bin_sum[...] = jnp.zeros_like(bin_sum)
    b_in = jnp.concatenate([bin_ref[part : part + 1] for part in range(H // LANES)], axis=1)
    gain, bias, bout, scale = gain_ref[...], bias_ref[...], bout_ref[...], scale_ref[...]
    count = ROWS * E * E

    def by_sublane(values):
        return jnp.sum(values.reshape(count // E, E, values.shape[1]), axis=0)

    def dense(step, carry):
        columns = pl.ds(step * ROWS, ROWS)
        rows = pl.ds(pl.multiple_of(step * count, count), count)
        conv_rows = conv[columns].reshape(count, C)
        row_mean = jnp.mean(conv_rows, axis=1, keepdims=True)
        centred = conv_rows - row_mean
        row_var = jnp.mean(centred * centred, axis=1, keepdims=True)
        inv_std = lax.rsqrt(row_var + NORM_EPS)
        unit_rows = centred * inv_std
        normed = (unit_rows * gain + bias).astype(BF16)
        pre_act = jnp.dot(normed, win_ref[...], preferred_element_type=F32) + b_in
        square = pre_act * pre_act
        tanh_value = jnp.tanh(GELU_SCALE * (pre_act + GELU_CUBIC * square * pre_act))
        half = 0.5 * (1.0 + tanh_value)
        activated = (pre_act * half).astype(BF16)
        slope = half + 0.5 * pre_act * (1.0 - tanh_value * tanh_value) * (
            GELU_SCALE * (1.0 + 3.0 * GELU_CUBIC * square)
        )
        branch = (
            lax.dot_general(
                activated, wout_ref[...], (((1,), (1,)), ((), ())), preferred_element_type=F32
            )
            + bout
        )
        mixed[columns] = (field[columns].reshape(count, C) + scale * branch).reshape(ROWS, E, E, C)
        seed = upstream[columns].reshape(count, C)
        grad_branch = (seed * scale).astype(BF16)
        grad_act = jnp.dot(grad_branch, wout_ref[...], preferred_element_type=F32)
        grad_pre = (grad_act * slope).astype(BF16)
        grad_normed = lax.dot_general(
            grad_pre, win_ref[...], (((1,), (1,)), ((), ())), preferred_element_type=F32
        )
        scaled = grad_normed * gain
        grad_conv = inv_std * (
            scaled
            - jnp.mean(scaled, axis=1, keepdims=True)
            - unit_rows * jnp.mean(scaled * unit_rows, axis=1, keepdims=True)
        )
        grad[columns] = grad_conv.astype(BF16).astype(F32).reshape(ROWS, E, E, C)
        normed_all[rows] = normed
        act_all[rows] = activated
        gpre_all[rows] = grad_pre
        gbranch_all[rows] = grad_branch
        vec_sum[0] += by_sublane(grad_normed * unit_rows)
        vec_sum[1] += by_sublane(grad_normed)
        vec_sum[2] += by_sublane(grad_branch.astype(F32))
        vec_sum[3] += by_sublane(seed * branch)
        bin_sum[...] += by_sublane(grad_pre.astype(F32))
        return carry

    lax.fori_loop(0, E // ROWS, dense, 0)

    def grad_rims(x, carry):
        grims[0, x] = grad[x, E - 2 :].reshape(2 * E, C).astype(BF16)
        grims[1, x] = grad[x, :2].reshape(2 * E, C).astype(BF16)
        return carry

    lax.fori_loop(0, E, grad_rims, 0)
    send(grims.at[0], ghalos.at[0], halo_send.at[2], halo_recv.at[2], above)
    send(grims.at[1], ghalos.at[1], halo_send.at[3], halo_recv.at[3], below)

    by_rows = (((0,), (0,)), ((), ()))
    for base, left, right in ((0, normed_all, gpre_all), (18, gbranch_all, act_all)):
        product = lax.dot_general(left[...], right[...], by_rows, preferred_element_type=F32)
        for part in range(H // LANES):
            piece = product[:, part * LANES : (part + 1) * LANES].astype(BF16)
            w_out1[base + 6 * part : base + 6 * part + 6] = piece.reshape(6, TILE, LANES)
    vec_tile[...] = jnp.zeros_like(vec_tile)
    bin_row = jnp.sum(bin_sum[...], axis=0, keepdims=True)
    for part in range(H // LANES):
        vec_tile[part : part + 1] = bin_row[:, part * LANES : (part + 1) * LANES]
    for row in range(4):
        vec_tile[3 + row : 4 + row, 0:C] = jnp.sum(vec_sum[row], axis=0, keepdims=True)
    w_out1[36] = vec_tile[...].astype(BF16)
    w_out1[37:W_TILES] = jnp.zeros((W_TILES - 37, TILE, LANES), BF16)
    send_all(
        x_peers, lambda peer: w_out1.at[pl.ds(peer * W_SHARE, W_SHARE)],
        lambda slot: w_in1.at[slot], send_sem.at[0], recv_sem.at[0],
    )

    kernel_rows[...] = jnp.zeros_like(kernel_rows)

    def kernel_pair(pair, carry):
        tap_z = pair // K
        tap_y = lax.rem(pair, K)
        sums = [jnp.zeros((E, C), F32) for _ in range(K)]
        for z in range(E):
            window = padded[tap_y, :, z + tap_z]
            factor = grad[:, z]
            for tap_x in range(K):
                sums[tap_x] = sums[tap_x] + jnp.sum(window[tap_x : tap_x + E] * factor, axis=0)
        for tap_x in range(K):
            total = jnp.sum(sums[tap_x], axis=0, keepdims=True)
            kernel_rows[pl.ds(pair * K + tap_x, 1), 0:C] = total
        return carry

    lax.fori_loop(0, K * K, kernel_pair, 0)
    k_out1[...] = kernel_rows[...].astype(BF16).reshape(K_TILES, TILE, LANES)
    send_all(
        x_peers, lambda peer: k_out1.at[pl.ds(peer * K_SHARE, K_SHARE)],
        lambda slot: k_in1.at[slot], send_sem.at[5], recv_sem.at[5],
    )

    def own_grad_column(x, carry):
        spread_own(gpadded, x, grad[x], y_index)
        return carry

    lax.fori_loop(0, E, own_grad_column, 0)

    wait_bytes(w_in1, recv_sem.at[0])
    total = add_all(w_out1[pl.ds(sample * W_SHARE, W_SHARE)], w_in1, NS - 1)
    w_out2[0:W_SHARE] = total.astype(BF16)
    if NY * PART > W_SHARE:
        w_out2[W_SHARE : NY * PART] = jnp.zeros((NY * PART - W_SHARE, TILE, LANES), BF16)
    send_all(
        y_peers, lambda peer: w_out2.at[pl.ds(peer * PART, PART)],
        lambda slot: w_in2.at[slot], send_sem.at[1], recv_sem.at[1],
    )

    conv_planes(gpadded, weights, conv, 2, 6, True)

    wait_bytes(k_in1, recv_sem.at[5])
    total = add_all(k_out1[pl.ds(sample * K_SHARE, K_SHARE)], k_in1, NS - 1)
    k_out2[...] = total.astype(BF16)
    send_all(
        y_peers, lambda peer: k_out2, lambda slot: k_in2.at[slot], send_sem.at[6], recv_sem.at[6]
    )

    wait_bytes(w_in2, recv_sem.at[1])
    total = add_all(w_out2[pl.ds(chip_y * PART, PART)], w_in2, NY - 1)
    w_out3[...] = total.astype(BF16)
    send_all(
        z_peers, lambda peer: w_out3, lambda slot: w_in3.at[slot], send_sem.at[2], recv_sem.at[2]
    )

    for side in range(2):
        wait_bytes(ghalos.at[side], halo_recv.at[2 + side])
    place_halos(gpadded, ghalos)

    wait_bytes(k_in2, recv_sem.at[6])
    k_out3[...] = add_all(k_out2[...], k_in2, NY - 1).astype(BF16)
    send_all(
        z_peers, lambda peer: k_out3, lambda slot: k_in3.at[slot], send_sem.at[7], recv_sem.at[7]
    )

    conv_planes(gpadded, weights, conv, 6, 10, True)

    for x in range(E):
        lanes = slice(x * C, (x + 1) * C)
        mixed_ref[:, :, lanes] = mixed[x].astype(BF16)
        gfield_ref[:, :, lanes] = (upstream[x] + conv[x] * fluid[x]).astype(BF16)
    stores[0].start()
    stores[1].start()

    wait_bytes(w_in3, recv_sem.at[2])
    mine = pl.ds(chip_y * PART, PART)
    w_share[mine] = add_all(w_out3[...], w_in3, NZ - 1).astype(BF16)
    send_all(
        y_peers, lambda peer: w_share.at[mine], lambda slot: w_share.at[mine],
        send_sem.at[3], recv_sem.at[3],
    )

    wait_bytes(k_in3, recv_sem.at[7])
    k_all[sample] = add_all(k_out3[...], k_in3, NZ - 1).astype(BF16)
    send_all(
        x_peers, lambda peer: k_all.at[sample], lambda slot: k_all.at[sample],
        send_sem.at[8], recv_sem.at[8],
    )

    wait_bytes(w_share.at[0 : (NY - 1) * PART], recv_sem.at[3])
    w_all[sample] = w_share[0:W_SHARE]
    send_all(
        x_peers, lambda peer: w_all.at[sample], lambda slot: w_all.at[sample],
        send_sem.at[4], recv_sem.at[4],
    )

    wait_bytes(k_all.at[0 : NS - 1], recv_sem.at[8])
    factor = 1.0 / math.sqrt(NS * layers * E**3)

    rows = k_all[...].astype(F32).reshape(K_TILES * TILE, LANES)[:, 0:C] * factor
    for pair in range(K * K):
        gkernel_ref[pair // K, pair % K] = rows[pair * K : (pair + 1) * K]
    stores[2].start()

    wait_bytes(w_all.at[0 : NS - 1], recv_sem.at[4])

    def tile_of(index):
        return w_all[index // W_SHARE, index % W_SHARE].astype(F32) * factor

    for part in range(H // LANES):
        lanes = slice(part * LANES, (part + 1) * LANES)
        for row in range(6):
            gwin_ref[row * TILE : (row + 1) * TILE, lanes] = tile_of(6 * part + row)
            gwout_ref[row * TILE : (row + 1) * TILE, lanes] = tile_of(18 + 6 * part + row)
    last = tile_of(36)
    for part in range(H // LANES):
        gbin_ref[part : part + 1] = last[part : part + 1]
    gvec_ref[...] = last[3:7, 0:C]
    for store in stores[3:]:
        store.start()

    for side in range(2):
        wait_bytes(rims.at[side], halo_send.at[side])
        wait_bytes(grims.at[side], halo_send.at[2 + side])
    sent = (
        w_in1, w_in2, w_in3, w_share.at[0 : (NY - 1) * PART], w_all.at[0 : NS - 1],
        k_in1, k_in2, k_in3, k_all.at[0 : NS - 1],
    )
    for index, ref in enumerate(sent):
        wait_bytes(ref, send_sem.at[index])
    for store in stores:
        store.wait()


def write_out(*refs):
    sources, dests, sem = refs[:7], refs[7:14], refs[14]
    copies = [pltpu.make_async_copy(a, b, sem.at[i]) for i, (a, b) in enumerate(zip(sources, dests))]
    for copy in copies:
        copy.start()
    for copy in copies:
        copy.wait()


def local(
    features, wall_mask, block_positions, dw_kernel, norm_gain, norm_bias, w_in, b_in, w_out, b_out,
    layer_scale, upstream,
):
    voxels = (E, E, E, C)
    spread = (K, E + 4, E + 4, E, C)
    rows = E**3
    hbm = pl.BlockSpec(memory_space=pltpu.HBM)
    outs = (
        jax.ShapeDtypeStruct((E, E, E * C), BF16),
        jax.ShapeDtypeStruct((E, E, E * C), BF16),
        jax.ShapeDtypeStruct((K, K, K, C), F32),
        jax.ShapeDtypeStruct((C, H), F32),
        jax.ShapeDtypeStruct((C, H), F32),
        jax.ShapeDtypeStruct((H // LANES, LANES), F32),
        jax.ShapeDtypeStruct((4, C), F32),
    )
    scratch = [
        pltpu.VMEM((K * K, K, E, C), F32),
        pltpu.VMEM(spread, F32),
        pltpu.VMEM(spread, F32),
        pltpu.VMEM(voxels, F32),
        pltpu.VMEM(voxels, F32),
        pltpu.VMEM(voxels, F32),
        pltpu.VMEM(voxels, F32),
        pltpu.VMEM(voxels, F32),
        pltpu.VMEM(voxels, F32),
        pltpu.VMEM((rows, C), BF16),
        pltpu.VMEM((rows, H), BF16),
        pltpu.VMEM((rows, H), BF16),
        pltpu.VMEM((rows, C), BF16),
        pltpu.VMEM((4, E, C), F32),
        pltpu.VMEM((E, H), F32),
        pltpu.VMEM((K_TILES * TILE, LANES), F32),
        pltpu.VMEM((TILE, LANES), F32),
        pltpu.VMEM((2, E, 2 * E, C), BF16),
        pltpu.VMEM((2, E, 2 * E, C), BF16),
        pltpu.VMEM((2, E, 2 * E, C), BF16),
        pltpu.VMEM((2, E, 2 * E, C), BF16),
        *(pltpu.VMEM((*lead, TILE, LANES), BF16) for lead in (
            (W_TILES,), (NS - 1, W_SHARE), (NY * PART,), (NY - 1, PART), (PART,), (NZ - 1, PART),
            (NY * PART,), (NS, W_SHARE),
            (K_TILES,), (NS - 1, K_SHARE), (K_SHARE,), (NY - 1, K_SHARE), (K_SHARE,),
            (NZ - 1, K_SHARE), (NS, K_SHARE),
        )),
        *(pltpu.VMEM(shape, dtype) for shape, dtype in (
            ((E, E, E * C), BF16), ((E, E * E), jnp.int32), ((1, NY * NZ), jnp.int32),
            ((K, K, K, C), F32), ((1, C), F32), ((1, C), F32), ((C, H), BF16),
            ((H // LANES, LANES), F32), ((C, H), BF16), ((1, C), F32), ((1, C), F32),
            ((E, E, E * C), BF16),
        )),
        *(pltpu.VMEM(out.shape, out.dtype) for out in outs),
        pltpu.SemaphoreType.DMA((4,)),
        pltpu.SemaphoreType.DMA((4,)),
        pltpu.SemaphoreType.DMA((9,)),
        pltpu.SemaphoreType.DMA((9,)),
        pltpu.SemaphoreType.DMA((12,)),
        pltpu.SemaphoreType.DMA((7,)),
    ]
    results = pl.pallas_call(
        body,
        out_shape=outs,
        in_specs=[hbm] * 12,
        out_specs=[hbm] * 7,
        scratch_shapes=scratch,
        compiler_params=pltpu.CompilerParams(
            collective_id=0, has_side_effects=True, vmem_limit_bytes=VMEM_BYTES
        ),
        cost_estimate=pl.CostEstimate(flops=400_000_000, bytes_accessed=1_500_000, transcendentals=200_000),
        name="block_step",
    )(
        features[0, 0, 0],
        wall_mask[0, 0, 0],
        block_positions[:, :, 0],
        dw_kernel,
        norm_gain[None],
        norm_bias[None],
        w_in,
        b_in.reshape(H // LANES, LANES),
        w_out.T,
        b_out[None],
        layer_scale[None],
        upstream[0, 0, 0],
    )
    results = pl.pallas_call(
        write_out,
        out_shape=outs,
        in_specs=[hbm] * 7,
        out_specs=[hbm] * 7,
        scratch_shapes=[pltpu.SemaphoreType.DMA((7,))],
        compiler_params=pltpu.CompilerParams(vmem_limit_bytes=VMEM_BYTES),
        cost_estimate=pl.CostEstimate(flops=0, bytes_accessed=1_000_000, transcendentals=0),
        name="write_results",
    )(*results)
    mixed, gfield, gkernel, gwin, gwout, gbin, gvec = results
    return (mixed[None, None, None], gfield[None, None, None], gkernel, gwin, gwout.T, gbin.reshape(H), gvec)


def solution(mesh):
    sharded = P("sample", "space", None, None, None, None)
    return jax.shard_map(
        local,
        mesh=mesh,
        in_specs=(
            sharded,
            P("sample", "space", None, None, None),
            P("sample", None, None),
            P(), P(), P(), P(), P(), P(), P(), P(),
            sharded,
        ),
        out_specs=(sharded, sharded, P(), P(), P(), P(), P()),
        check_vma=False,
    )
```

```python
import math

import jax
import jax.numpy as jnp
from jax import lax
from jax.experimental import pallas as pl
from jax.experimental.pallas import tpu as pltpu
from jax.sharding import PartitionSpec as P

F32 = jnp.float32
BF16 = jnp.bfloat16
MESH = pl.DeviceIdType.MESH

GELU_SCALE = 0.7978845608028654
GELU_CUBIC = 0.044715
NORM_EPS = 1e-06

VMEM_BYTES = 62 * 1024 * 1024
E = 8
K = 5
C = 96
H = 384
NZ = 16
NY = 8
NS = 8
ROWS = 8
TILE = 16
LANES = 128
W_TILES = 40
K_TILES = 8
W_SHARE = W_TILES // NS
K_SHARE = K_TILES // NS
PART = -(-W_SHARE // NY)


def wait_bytes(ref, sem):
    pltpu.make_async_copy(ref, ref, sem).wait()


def send(src, dst, send_sem, recv_sem, device):
    pltpu.make_async_remote_copy(
        src_ref=src,
        dst_ref=dst,
        send_sem=send_sem,
        recv_sem=recv_sem,
        device_id=device,
        device_id_type=MESH,
    ).start()


def ring_order(count):
    return sorted(range(1, count), key=lambda step: -min(step, count - step))


def sample_order():
    chips = NS // 2
    steps = [(x, core) for x in range(chips) for core in range(2) if (x, core) != (0, 0)]
    return sorted(steps, key=lambda step: -min(step[0], chips - step[0]))


def send_all(peers, src, dst, send_sem, recv_sem):
    for slot, (index, device) in enumerate(peers):
        send(src(index), dst(slot), send_sem, recv_sem, device)


def add_all(total, parts, count):
    total = total.astype(F32)
    for slot in range(count):
        total = total + parts[slot].astype(F32)
    return total


def axis_region(index):
    return jnp.where(index < 2, -1, jnp.where(index < 2 + E, 0, 1))


def shifted(block, tap):
    return pltpu.roll(block, (2 - tap) % E, 1)


def spread_own(dest, column, block, y_index):
    for tap in range(K):
        keep = (axis_region(y_index + tap) == 0).astype(F32)
        dest[tap, column + 2, 2 : 2 + E] = shifted(block, tap) * keep


def clear_sides(dest):
    dest[:, 0:2, 2 : 2 + E] = jnp.zeros((K, 2, E, E, C), F32)
    dest[:, 2 + E : 4 + E, 2 : 2 + E] = jnp.zeros((K, 2, E, E, C), F32)
    dest[:, :, 0:2] = jnp.zeros((K, E + 4, 2, E, C), F32)
    dest[:, :, 2 + E : 4 + E] = jnp.zeros((K, E + 4, 2, E, C), F32)


def spread_halo(dest, halo, low, step_y, step_x, exists, y_index):
    for tap in range(K):
        keep_y = (axis_region(y_index + tap) == step_y) & exists
        for region in (-1, 0, 1):
            keep = (keep_y & (step_x == region)).astype(F32)
            first, count = {-1: (0, 2), 0: (2, E), 1: (2 + E, 2)}[region]
            source = (first + E - 2) % E
            block = halo[source : source + count].astype(F32).reshape(count * 2, E, C)
            block = shifted(block, tap).reshape(count, 2, E, C) * keep
            dest[tap, first : first + count, low : low + 2] = block


def tap_row(weights, tap_z, tap_y, tap_x, reverse):
    pair = tap_z * K + tap_y
    return weights[K * K - 1 - pair, K - 1 - tap_x] if reverse else weights[pair, tap_x]


def plane_sum(field, weights, total, z, tap_z, reverse):
    for tap_y in range(K):
        window = field[tap_y, :, z + tap_z]
        for tap_x in range(K):
            row = tap_row(weights, tap_z, tap_y, tap_x, reverse)
            total = total + window[tap_x : tap_x + E] * row
    return total


def conv_own(field, weights, out, reverse):
    def plane(z, carry):
        total = jnp.zeros((E, E, C), F32)
        for tap_z in range(K):
            total = plane_sum(field, weights, total, z, tap_z, reverse)
        out[:, z] = total
        return carry

    lax.fori_loop(0, E, plane, 0)


def conv_halo(field, weights, out, reverse):
    for z, taps in ((0, (0, 1)), (1, (0,)), (6, (4,)), (7, (3, 4))):
        total = out[:, z]
        for tap_z in taps:
            total = plane_sum(field, weights, total, z, tap_z, reverse)
        out[:, z] = total


def body(
    field_hbm, wall_hbm, pos_hbm, dw_hbm, gain_hbm, bias_hbm, win_hbm, bin_hbm, wout_hbm, bout_hbm,
    scale_hbm, up_hbm,
    mixed_hbm, gfield_hbm, gkernel_hbm, gwin_hbm, gwout_hbm, gbin_hbm, gvec_hbm,
    weights, padded, gpadded, conv, grad, fluid, field, upstream, mixed,
    normed_all, act_all, gpre_all, gbranch_all, vec_sum, bin_sum, kernel_rows, vec_tile,
    rims, halos, grims, ghalos,
    w_out1, w_in1, w_out2, w_in2, w_out3, w_in3, w_share, w_all,
    k_out1, k_in1, k_out2, k_in2, k_out3, k_in3, k_all,
    field_ref, wall_ref, pos_ref, dw_ref, gain_ref, bias_ref, win_ref, bin_ref, wout_ref, bout_ref,
    scale_ref, up_ref,
    mixed_ref, gfield_ref, gkernel_ref, gwin_ref, gwout_ref, gbin_ref, gvec_ref,
    halo_send, halo_recv, send_sem, recv_sem, load_sem, store_sem,
):
    stores = [
        pltpu.make_async_copy(source, dest, store_sem.at[index])
        for index, (source, dest) in enumerate((
            (mixed_ref, mixed_hbm), (gfield_ref, gfield_hbm), (gkernel_ref, gkernel_hbm),
            (gwin_ref, gwin_hbm), (gwout_ref, gwout_hbm), (gbin_ref, gbin_hbm), (gvec_ref, gvec_hbm),
        ))
    ]
    loads = [
        pltpu.make_async_copy(source, dest, load_sem.at[index])
        for index, (source, dest) in enumerate((
            (field_hbm, field_ref), (wall_hbm, wall_ref), (dw_hbm, dw_ref), (up_hbm, up_ref),
            (pos_hbm, pos_ref), (gain_hbm, gain_ref), (bias_hbm, bias_ref), (win_hbm, win_ref),
            (bin_hbm, bin_ref), (wout_hbm, wout_ref), (bout_hbm, bout_ref), (scale_hbm, scale_ref),
        ))
    ]
    for load in loads:
        load.start()
    space = lax.axis_index("space")
    sample = lax.axis_index("sample")
    layers = NY * NZ
    chip_y = space // NZ
    chip_z = lax.rem(space, NZ)
    above = (lax.rem(space + 1, layers), sample)
    below = (lax.rem(space + layers - 1, layers), sample)

    x_peers = []
    for step_x, step_core in sample_order():
        x = lax.rem(sample // 2 + step_x, NS // 2)
        index = x * 2 + lax.rem(sample + step_core, 2)
        x_peers.append((index, (space, index)))
    y_peers = []
    for step in ring_order(NY):
        index = lax.rem(chip_y + step, NY)
        y_peers.append((index, (index * NZ + chip_z, sample)))
    z_peers = []
    for step in ring_order(NZ):
        index = lax.rem(chip_z + step, NZ)
        z_peers.append((index, (chip_y * NZ + index, sample)))

    barrier = pltpu.get_barrier_semaphore()
    partners = [above, below] + [device for _, device in x_peers + y_peers + z_peers]
    for device in partners:
        pl.semaphore_signal(barrier, inc=1, device_id=device, device_id_type=MESH)

    loads[0].wait()
    loads[1].wait()
    y_index = lax.broadcasted_iota(jnp.int32, (E, C), 0)
    lane = lax.broadcasted_iota(jnp.int32, (E, E, E * E), 2)
    sub = lax.broadcasted_iota(jnp.int32, (E, E, E * E), 1)
    walls = jnp.broadcast_to(wall_ref[...].astype(F32)[:, None, :], (E, E, E * E))
    walls = jnp.where(lane // E == sub, walls, 0.0).reshape(E * E, E * E).astype(BF16)
    voxel = lax.broadcasted_iota(jnp.int32, (E * E, C), 0)
    wide = field_ref[...].astype(F32)
    for x in range(E):
        pick = (lax.rem(voxel, E) == x).astype(BF16)
        open_x = 1.0 - jnp.dot(walls, pick, preferred_element_type=F32)
        fluid[x] = open_x.reshape(E, E, C)
        column = wide[:, :, x * C : (x + 1) * C]
        field[x] = column
        masked = column * fluid[x]
        conv[x] = masked
        rims[0, x] = masked[E - 2 :].reshape(2 * E, C).astype(BF16)
        rims[1, x] = masked[:2].reshape(2 * E, C).astype(BF16)

    clear_sides(padded)

    def own_column(x, carry):
        spread_own(padded, x, conv[x], y_index)
        return carry

    lax.fori_loop(0, E, own_column, 0)
    loads[2].wait()

    def spread_weights(pair, carry):
        rows = dw_ref[pair // K, lax.rem(pair, K)]
        weights[pair] = jnp.broadcast_to(rows[:, None, :], (K, E, C))
        return carry

    lax.fori_loop(0, K * K, spread_weights, 0)
    conv_own(padded, weights, conv, False)

    pl.semaphore_wait(barrier, len(partners))
    send(rims.at[0], halos.at[0], halo_send.at[0], halo_recv.at[0], above)
    send(rims.at[1], halos.at[1], halo_send.at[1], halo_recv.at[1], below)

    for load in loads[3:]:
        load.wait()
    wide = up_ref[...].astype(F32)
    for x in range(E):
        upstream[x] = wide[:, :, x * C : (x + 1) * C]
    clear_sides(gpadded)

    layer_index = lax.broadcasted_iota(jnp.int32, (1, layers), 1)

    def position(layer):
        return jnp.sum(jnp.where(layer_index == layer, pos_ref[...], 0), axis=1, keepdims=True)

    own_pos, low_pos, high_pos = position(space), position(space - 1), position(space + 1)
    step_low = (low_pos // 2 - own_pos // 2, low_pos % 2 - own_pos % 2)
    step_high = (high_pos // 2 - own_pos // 2, high_pos % 2 - own_pos % 2)

    def place_halos(dest, received):
        spread_halo(dest, received.at[0], 0, *step_low, space > 0, y_index)
        spread_halo(dest, received.at[1], 2 + E, *step_high, space < layers - 1, y_index)

    for side in range(2):
        wait_bytes(halos.at[side], halo_recv.at[side])
    place_halos(padded, halos)
    conv_halo(padded, weights, conv, False)

    vec_sum[...] = jnp.zeros_like(vec_sum)
    bin_sum[...] = jnp.zeros_like(bin_sum)
    b_in = jnp.concatenate([bin_ref[part : part + 1] for part in range(H // LANES)], axis=1)
    gain, bias, bout, scale = gain_ref[...], bias_ref[...], bout_ref[...], scale_ref[...]
    count = ROWS * E * E

    def by_sublane(values):
        return jnp.sum(values.reshape(count // E, E, values.shape[1]), axis=0)

    def dense(step, carry):
        columns = pl.ds(step * ROWS, ROWS)
        rows = pl.ds(pl.multiple_of(step * count, count), count)
        conv_rows = conv[columns].reshape(count, C)
        row_mean = jnp.mean(conv_rows, axis=1, keepdims=True)
        centred = conv_rows - row_mean
        row_var = jnp.mean(centred * centred, axis=1, keepdims=True)
        inv_std = lax.rsqrt(row_var + NORM_EPS)
        unit_rows = centred * inv_std
        normed = (unit_rows * gain + bias).astype(BF16)
        pre_act = jnp.dot(normed, win_ref[...], preferred_element_type=F32) + b_in
        square = pre_act * pre_act
        tanh_value = jnp.tanh(GELU_SCALE * (pre_act + GELU_CUBIC * square * pre_act))
        half = 0.5 * (1.0 + tanh_value)
        activated = (pre_act * half).astype(BF16)
        slope = half + 0.5 * pre_act * (1.0 - tanh_value * tanh_value) * (
            GELU_SCALE * (1.0 + 3.0 * GELU_CUBIC * square)
        )
        branch = (
            lax.dot_general(
                activated, wout_ref[...], (((1,), (1,)), ((), ())), preferred_element_type=F32
            )
            + bout
        )
        mixed[columns] = (field[columns].reshape(count, C) + scale * branch).reshape(ROWS, E, E, C)
        seed = upstream[columns].reshape(count, C)
        grad_branch = (seed * scale).astype(BF16)
        grad_act = jnp.dot(grad_branch, wout_ref[...], preferred_element_type=F32)
        grad_pre = (grad_act * slope).astype(BF16)
        grad_normed = lax.dot_general(
            grad_pre, win_ref[...], (((1,), (1,)), ((), ())), preferred_element_type=F32
        )
        scaled = grad_normed * gain
        grad_conv = inv_std * (
            scaled
            - jnp.mean(scaled, axis=1, keepdims=True)
            - unit_rows * jnp.mean(scaled * unit_rows, axis=1, keepdims=True)
        )
        grad[columns] = grad_conv.astype(BF16).astype(F32).reshape(ROWS, E, E, C)
        normed_all[rows] = normed
        act_all[rows] = activated
        gpre_all[rows] = grad_pre
        gbranch_all[rows] = grad_branch
        vec_sum[0] += by_sublane(grad_normed * unit_rows)
        vec_sum[1] += by_sublane(grad_normed)
        vec_sum[2] += by_sublane(grad_branch.astype(F32))
        vec_sum[3] += by_sublane(seed * branch)
        bin_sum[...] += by_sublane(grad_pre.astype(F32))
        return carry

    lax.fori_loop(0, E // ROWS, dense, 0)

    def grad_rims(x, carry):
        grims[0, x] = grad[x, E - 2 :].reshape(2 * E, C).astype(BF16)
        grims[1, x] = grad[x, :2].reshape(2 * E, C).astype(BF16)
        return carry

    lax.fori_loop(0, E, grad_rims, 0)
    send(grims.at[0], ghalos.at[0], halo_send.at[2], halo_recv.at[2], above)
    send(grims.at[1], ghalos.at[1], halo_send.at[3], halo_recv.at[3], below)

    by_rows = (((0,), (0,)), ((), ()))
    for base, left, right in ((0, normed_all, gpre_all), (18, gbranch_all, act_all)):
        product = lax.dot_general(left[...], right[...], by_rows, preferred_element_type=F32)
        for part in range(H // LANES):
            piece = product[:, part * LANES : (part + 1) * LANES].astype(BF16)
            w_out1[base + 6 * part : base + 6 * part + 6] = piece.reshape(6, TILE, LANES)
    vec_tile[...] = jnp.zeros_like(vec_tile)
    bin_row = jnp.sum(bin_sum[...], axis=0, keepdims=True)
    for part in range(H // LANES):
        vec_tile[part : part + 1] = bin_row[:, part * LANES : (part + 1) * LANES]
    for row in range(4):
        vec_tile[3 + row : 4 + row, 0:C] = jnp.sum(vec_sum[row], axis=0, keepdims=True)
    w_out1[36] = vec_tile[...].astype(BF16)
    w_out1[37:W_TILES] = jnp.zeros((W_TILES - 37, TILE, LANES), BF16)
    send_all(
        x_peers, lambda peer: w_out1.at[pl.ds(peer * W_SHARE, W_SHARE)],
        lambda slot: w_in1.at[slot], send_sem.at[0], recv_sem.at[0],
    )

    kernel_rows[...] = jnp.zeros_like(kernel_rows)

    def kernel_pair(pair, carry):
        tap_z = pair // K
        tap_y = lax.rem(pair, K)
        sums = [jnp.zeros((E, C), F32) for _ in range(K)]
        for z in range(E):
            window = padded[tap_y, :, z + tap_z]
            factor = grad[:, z]
            for tap_x in range(K):
                sums[tap_x] = sums[tap_x] + jnp.sum(window[tap_x : tap_x + E] * factor, axis=0)
        for tap_x in range(K):
            total = jnp.sum(sums[tap_x], axis=0, keepdims=True)
            kernel_rows[pl.ds(pair * K + tap_x, 1), 0:C] = total
        return carry

    lax.fori_loop(0, K * K, kernel_pair, 0)
    k_out1[...] = kernel_rows[...].astype(BF16).reshape(K_TILES, TILE, LANES)
    send_all(
        x_peers, lambda peer: k_out1.at[pl.ds(peer * K_SHARE, K_SHARE)],
        lambda slot: k_in1.at[slot], send_sem.at[5], recv_sem.at[5],
    )

    def own_grad_column(x, carry):
        spread_own(gpadded, x, grad[x], y_index)
        return carry

    lax.fori_loop(0, E, own_grad_column, 0)

    wait_bytes(w_in1, recv_sem.at[0])
    total = add_all(w_out1[pl.ds(sample * W_SHARE, W_SHARE)], w_in1, NS - 1)
    w_out2[0:W_SHARE] = total.astype(BF16)
    if NY * PART > W_SHARE:
        w_out2[W_SHARE : NY * PART] = jnp.zeros((NY * PART - W_SHARE, TILE, LANES), BF16)
    send_all(
        y_peers, lambda peer: w_out2.at[pl.ds(peer * PART, PART)],
        lambda slot: w_in2.at[slot], send_sem.at[1], recv_sem.at[1],
    )

    conv_own(gpadded, weights, conv, True)

    wait_bytes(k_in1, recv_sem.at[5])
    total = add_all(k_out1[pl.ds(sample * K_SHARE, K_SHARE)], k_in1, NS - 1)
    k_out2[...] = total.astype(BF16)
    send_all(
        y_peers, lambda peer: k_out2, lambda slot: k_in2.at[slot], send_sem.at[6], recv_sem.at[6]
    )

    wait_bytes(w_in2, recv_sem.at[1])
    total = add_all(w_out2[pl.ds(chip_y * PART, PART)], w_in2, NY - 1)
    w_out3[...] = total.astype(BF16)
    send_all(
        z_peers, lambda peer: w_out3, lambda slot: w_in3.at[slot], send_sem.at[2], recv_sem.at[2]
    )

    for side in range(2):
        wait_bytes(ghalos.at[side], halo_recv.at[2 + side])
    place_halos(gpadded, ghalos)

    wait_bytes(k_in2, recv_sem.at[6])
    k_out3[...] = add_all(k_out2[...], k_in2, NY - 1).astype(BF16)
    send_all(
        z_peers, lambda peer: k_out3, lambda slot: k_in3.at[slot], send_sem.at[7], recv_sem.at[7]
    )

    conv_halo(gpadded, weights, conv, True)

    for x in range(E):
        lanes = slice(x * C, (x + 1) * C)
        mixed_ref[:, :, lanes] = mixed[x].astype(BF16)
        gfield_ref[:, :, lanes] = (upstream[x] + conv[x] * fluid[x]).astype(BF16)
    stores[0].start()
    stores[1].start()

    wait_bytes(w_in3, recv_sem.at[2])
    mine = pl.ds(chip_y * PART, PART)
    w_share[mine] = add_all(w_out3[...], w_in3, NZ - 1).astype(BF16)
    send_all(
        y_peers, lambda peer: w_share.at[mine], lambda slot: w_share.at[mine],
        send_sem.at[3], recv_sem.at[3],
    )

    wait_bytes(k_in3, recv_sem.at[7])
    k_all[sample] = add_all(k_out3[...], k_in3, NZ - 1).astype(BF16)
    send_all(
        x_peers, lambda peer: k_all.at[sample], lambda slot: k_all.at[sample],
        send_sem.at[8], recv_sem.at[8],
    )

    wait_bytes(w_share.at[0 : (NY - 1) * PART], recv_sem.at[3])
    w_all[sample] = w_share[0:W_SHARE]
    send_all(
        x_peers, lambda peer: w_all.at[sample], lambda slot: w_all.at[sample],
        send_sem.at[4], recv_sem.at[4],
    )

    wait_bytes(k_all.at[0 : NS - 1], recv_sem.at[8])
    factor = 1.0 / math.sqrt(NS * layers * E**3)

    rows = k_all[...].astype(F32).reshape(K_TILES * TILE, LANES)[:, 0:C] * factor
    for pair in range(K * K):
        gkernel_ref[pair // K, pair % K] = rows[pair * K : (pair + 1) * K]
    stores[2].start()

    wait_bytes(w_all.at[0 : NS - 1], recv_sem.at[4])

    def tile_of(index):
        return w_all[index // W_SHARE, index % W_SHARE].astype(F32) * factor

    for part in range(H // LANES):
        lanes = slice(part * LANES, (part + 1) * LANES)
        for row in range(6):
            gwin_ref[row * TILE : (row + 1) * TILE, lanes] = tile_of(6 * part + row)
            gwout_ref[row * TILE : (row + 1) * TILE, lanes] = tile_of(18 + 6 * part + row)
    last = tile_of(36)
    for part in range(H // LANES):
        gbin_ref[part : part + 1] = last[part : part + 1]
    gvec_ref[...] = last[3:7, 0:C]
    for store in stores[3:]:
        store.start()

    for side in range(2):
        wait_bytes(rims.at[side], halo_send.at[side])
        wait_bytes(grims.at[side], halo_send.at[2 + side])
    sent = (
        w_in1, w_in2, w_in3, w_share.at[0 : (NY - 1) * PART], w_all.at[0 : NS - 1],
        k_in1, k_in2, k_in3, k_all.at[0 : NS - 1],
    )
    for index, ref in enumerate(sent):
        wait_bytes(ref, send_sem.at[index])
    for store in stores:
        store.wait()


def write_out(*refs):
    sources, dests, held, sem = refs[:7], refs[7:14], refs[14:21], refs[21]
    loads = [pltpu.make_async_copy(a, b, sem.at[0, i]) for i, (a, b) in enumerate(zip(sources, held))]
    stores = [pltpu.make_async_copy(a, b, sem.at[1, i]) for i, (a, b) in enumerate(zip(held, dests))]
    for load in loads:
        load.start()
    for load, store in zip(loads, stores):
        load.wait()
        store.start()
    for store in stores:
        store.wait()


def local(
    features, wall_mask, block_positions, dw_kernel, norm_gain, norm_bias, w_in, b_in, w_out, b_out,
    layer_scale, upstream,
):
    voxels = (E, E, E, C)
    spread = (K, E + 4, E + 4, E, C)
    rows = E**3
    hbm = pl.BlockSpec(memory_space=pltpu.HBM)
    outs = (
        jax.ShapeDtypeStruct((E, E, E * C), BF16),
        jax.ShapeDtypeStruct((E, E, E * C), BF16),
        jax.ShapeDtypeStruct((K, K, K, C), F32),
        jax.ShapeDtypeStruct((C, H), F32),
        jax.ShapeDtypeStruct((C, H), F32),
        jax.ShapeDtypeStruct((H // LANES, LANES), F32),
        jax.ShapeDtypeStruct((4, C), F32),
    )
    scratch = [
        pltpu.VMEM((K * K, K, E, C), F32),
        pltpu.VMEM(spread, F32),
        pltpu.VMEM(spread, F32),
        pltpu.VMEM(voxels, F32),
        pltpu.VMEM(voxels, F32),
        pltpu.VMEM(voxels, F32),
        pltpu.VMEM(voxels, F32),
        pltpu.VMEM(voxels, F32),
        pltpu.VMEM(voxels, F32),
        pltpu.VMEM((rows, C), BF16),
        pltpu.VMEM((rows, H), BF16),
        pltpu.VMEM((rows, H), BF16),
        pltpu.VMEM((rows, C), BF16),
        pltpu.VMEM((4, E, C), F32),
        pltpu.VMEM((E, H), F32),
        pltpu.VMEM((K_TILES * TILE, LANES), F32),
        pltpu.VMEM((TILE, LANES), F32),
        pltpu.VMEM((2, E, 2 * E, C), BF16),
        pltpu.VMEM((2, E, 2 * E, C), BF16),
        pltpu.VMEM((2, E, 2 * E, C), BF16),
        pltpu.VMEM((2, E, 2 * E, C), BF16),
        *(pltpu.VMEM((*lead, TILE, LANES), BF16) for lead in (
            (W_TILES,), (NS - 1, W_SHARE), (NY * PART,), (NY - 1, PART), (PART,), (NZ - 1, PART),
            (NY * PART,), (NS, W_SHARE),
            (K_TILES,), (NS - 1, K_SHARE), (K_SHARE,), (NY - 1, K_SHARE), (K_SHARE,),
            (NZ - 1, K_SHARE), (NS, K_SHARE),
        )),
        *(pltpu.VMEM(shape, dtype) for shape, dtype in (
            ((E, E, E * C), BF16), ((E, E * E), jnp.int32), ((1, NY * NZ), jnp.int32),
            ((K, K, K, C), F32), ((1, C), F32), ((1, C), F32), ((C, H), BF16),
            ((H // LANES, LANES), F32), ((C, H), BF16), ((1, C), F32), ((1, C), F32),
            ((E, E, E * C), BF16),
        )),
        *(pltpu.VMEM(out.shape, out.dtype) for out in outs),
        pltpu.SemaphoreType.DMA((4,)),
        pltpu.SemaphoreType.DMA((4,)),
        pltpu.SemaphoreType.DMA((9,)),
        pltpu.SemaphoreType.DMA((9,)),
        pltpu.SemaphoreType.DMA((12,)),
        pltpu.SemaphoreType.DMA((7,)),
    ]
    results = pl.pallas_call(
        body,
        out_shape=outs,
        in_specs=[hbm] * 12,
        out_specs=[hbm] * 7,
        scratch_shapes=scratch,
        compiler_params=pltpu.CompilerParams(
            collective_id=0, has_side_effects=True, vmem_limit_bytes=VMEM_BYTES
        ),
        cost_estimate=pl.CostEstimate(flops=400_000_000, bytes_accessed=1_500_000, transcendentals=200_000),
        name="block_step",
    )(
        features[0, 0, 0],
        wall_mask[0, 0, 0],
        block_positions[:, :, 0],
        dw_kernel,
        norm_gain[None],
        norm_bias[None],
        w_in,
        b_in.reshape(H // LANES, LANES),
        w_out.T,
        b_out[None],
        layer_scale[None],
        upstream[0, 0, 0],
    )
    results = pl.pallas_call(
        write_out,
        out_shape=outs,
        in_specs=[hbm] * 7,
        out_specs=[hbm] * 7,
        scratch_shapes=[
            *(pltpu.VMEM(out.shape, out.dtype) for out in outs),
            pltpu.SemaphoreType.DMA((2, 7)),
        ],
        compiler_params=pltpu.CompilerParams(vmem_limit_bytes=VMEM_BYTES),
        cost_estimate=pl.CostEstimate(flops=0, bytes_accessed=1_000_000, transcendentals=0),
        name="write_results",
    )(*results)
    mixed, gfield, gkernel, gwin, gwout, gbin, gvec = results
    return (mixed[None, None, None], gfield[None, None, None], gkernel, gwin, gwout.T, gbin.reshape(H), gvec)


def solution(mesh):
    sharded = P("sample", "space", None, None, None, None)
    return jax.shard_map(
        local,
        mesh=mesh,
        in_specs=(
            sharded,
            P("sample", "space", None, None, None),
            P("sample", None, None),
            P(), P(), P(), P(), P(), P(), P(), P(),
            sharded,
        ),
        out_specs=(sharded, sharded, P(), P(), P(), P(), P()),
        check_vma=False,
    )
```

```python
import math

import jax
import jax.numpy as jnp
from jax import lax
from jax.experimental import pallas as pl
from jax.experimental.pallas import tpu as pltpu
from jax.sharding import PartitionSpec as P

F32 = jnp.float32
BF16 = jnp.bfloat16
MESH = pl.DeviceIdType.MESH

GELU_SCALE = 0.7978845608028654
GELU_CUBIC = 0.044715
NORM_EPS = 1e-06

VMEM_BYTES = 62 * 1024 * 1024
E = 8
K = 5
C = 96
H = 384
NZ = 16
NY = 8
NS = 8
ROWS = 8
TILE = 16
LANES = 128
W_TILES = 40
K_TILES = 8
W_SHARE = W_TILES // NS
K_SHARE = K_TILES // NS
PART = -(-W_SHARE // NY)


def wait_bytes(ref, sem):
    pltpu.make_async_copy(ref, ref, sem).wait()


def send(src, dst, send_sem, recv_sem, device):
    pltpu.make_async_remote_copy(
        src_ref=src,
        dst_ref=dst,
        send_sem=send_sem,
        recv_sem=recv_sem,
        device_id=device,
        device_id_type=MESH,
    ).start()


def ring_order(count):
    return sorted(range(1, count), key=lambda step: -min(step, count - step))


def sample_order():
    chips = NS // 2
    steps = [(x, core) for x in range(chips) for core in range(2) if (x, core) != (0, 0)]
    return sorted(steps, key=lambda step: -min(step[0], chips - step[0]))


def send_all(peers, src, dst, send_sem, recv_sem):
    for slot, (index, device) in enumerate(peers):
        send(src(index), dst(slot), send_sem, recv_sem, device)


def add_all(total, parts, count):
    total = total.astype(F32)
    for slot in range(count):
        total = total + parts[slot].astype(F32)
    return total


def axis_region(index):
    return jnp.where(index < 2, -1, jnp.where(index < 2 + E, 0, 1))


def shifted(block, tap):
    return pltpu.roll(block, (2 - tap) % E, 1)


def spread_own(dest, column, block, y_index):
    for tap in range(K):
        keep = (axis_region(y_index + tap) == 0).astype(F32)
        dest[tap, column + 2, 2 : 2 + E] = shifted(block, tap) * keep


def clear_sides(dest):
    dest[:, 0:2, 2 : 2 + E] = jnp.zeros((K, 2, E, E, C), F32)
    dest[:, 2 + E : 4 + E, 2 : 2 + E] = jnp.zeros((K, 2, E, E, C), F32)


def spread_halo(dest, halo, low, step_y, step_x, exists, y_index):
    for tap in range(K):
        keep_y = (axis_region(y_index + tap) == step_y) & exists
        for region in (-1, 0, 1):
            keep = (keep_y & (step_x == region)).astype(F32)
            first, count = {-1: (0, 2), 0: (2, E), 1: (2 + E, 2)}[region]
            source = (first + E - 2) % E
            block = halo[source : source + count].astype(F32).reshape(count * 2, E, C)
            block = shifted(block, tap).reshape(count, 2, E, C) * keep
            dest[tap, first : first + count, low : low + 2] = block


def tap_row(weights, tap_z, tap_y, tap_x, reverse):
    pair = tap_z * K + tap_y
    return weights[K * K - 1 - pair, K - 1 - tap_x] if reverse else weights[pair, tap_x]


def plane_sum(field, weights, total, z, tap_z, reverse):
    for tap_y in range(K):
        window = field[tap_y, :, z + tap_z]
        for tap_x in range(K):
            row = tap_row(weights, tap_z, tap_y, tap_x, reverse)
            total = total + window[tap_x : tap_x + E] * row
    return total


def conv_own(field, weights, out, reverse):
    def tap_layer(tap_z, first):
        def plane(z, carry):
            totals = [None] * E
            for tap_y in range(K):
                window = field[tap_y, 2 : 2 + E, z + tap_z]
                for tap_x in range(K):
                    row = tap_row(weights, tap_z, tap_y, tap_x, reverse)
                    for x in range(max(0, 2 - tap_x), min(E, E + 2 - tap_x)):
                        term = window[x + tap_x - 2] * row
                        totals[x] = term if totals[x] is None else totals[x] + term
            for x in range(E):
                out[x, z] = totals[x] if first else out[x, z] + totals[x]
            return carry

        lax.fori_loop(max(0, 2 - tap_z), min(E, E + 2 - tap_z), plane, 0)

    for tap_z in (2, 0, 1, 3, 4):
        tap_layer(tap_z, tap_z == 2)


def conv_halo(field, weights, out, reverse):
    for z, taps in ((0, (0, 1)), (1, (0,)), (6, (4,)), (7, (3, 4))):
        total = out[:, z]
        for tap_z in taps:
            total = plane_sum(field, weights, total, z, tap_z, reverse)
        out[:, z] = total


def body(
    field_hbm, wall_hbm, pos_hbm, dw_hbm, gain_hbm, bias_hbm, win_hbm, bin_hbm, wout_hbm, bout_hbm,
    scale_hbm, up_hbm,
    mixed_hbm, gfield_hbm, gkernel_hbm, gwin_hbm, gwout_hbm, gbin_hbm, gvec_hbm,
    weights, padded, gpadded, conv, grad, fluid, field, upstream, mixed,
    normed_all, act_all, gpre_all, gbranch_all, vec_sum, bin_sum, kernel_rows, vec_tile,
    rims, halos, grims, ghalos,
    w_out1, w_in1, w_out2, w_in2, w_out3, w_in3, w_share, w_all,
    k_out1, k_in1, k_out2, k_in2, k_out3, k_in3, k_all,
    field_ref, wall_ref, pos_ref, dw_ref, gain_ref, bias_ref, win_ref, bin_ref, wout_ref, bout_ref,
    scale_ref, up_ref,
    mixed_ref, gfield_ref, gkernel_ref, gwin_ref, gwout_ref, gbin_ref, gvec_ref,
    halo_send, halo_recv, send_sem, recv_sem, load_sem, store_sem, ready,
):
    stores = [
        pltpu.make_async_copy(source, dest, store_sem.at[index])
        for index, (source, dest) in enumerate((
            (mixed_ref, mixed_hbm), (gfield_ref, gfield_hbm), (gkernel_ref, gkernel_hbm),
            (gwin_ref, gwin_hbm), (gwout_ref, gwout_hbm), (gbin_ref, gbin_hbm), (gvec_ref, gvec_hbm),
        ))
    ]
    loads = [
        pltpu.make_async_copy(source, dest, load_sem.at[index])
        for index, (source, dest) in enumerate((
            (field_hbm, field_ref), (wall_hbm, wall_ref), (dw_hbm, dw_ref), (up_hbm, up_ref),
            (pos_hbm, pos_ref), (gain_hbm, gain_ref), (bias_hbm, bias_ref), (win_hbm, win_ref),
            (bin_hbm, bin_ref), (wout_hbm, wout_ref), (bout_hbm, bout_ref), (scale_hbm, scale_ref),
        ))
    ]
    for load in loads:
        load.start()
    space = lax.axis_index("space")
    sample = lax.axis_index("sample")
    layers = NY * NZ
    chip_y = space // NZ
    chip_z = lax.rem(space, NZ)
    above = (lax.rem(space + 1, layers), sample)
    below = (lax.rem(space + layers - 1, layers), sample)

    x_peers = []
    for step_x, step_core in sample_order():
        x = lax.rem(sample // 2 + step_x, NS // 2)
        index = x * 2 + lax.rem(sample + step_core, 2)
        x_peers.append((index, (space, index)))
    y_peers = []
    for step in ring_order(NY):
        index = lax.rem(chip_y + step, NY)
        y_peers.append((index, (index * NZ + chip_z, sample)))
    z_peers = []
    for step in ring_order(NZ):
        index = lax.rem(chip_z + step, NZ)
        z_peers.append((index, (chip_y * NZ + index, sample)))

    def ring_pair(distance):
        pair = []
        if distance < NZ // 2:
            for step in (distance, NZ - distance):
                pair.append((chip_y * NZ + lax.rem(chip_z + step, NZ), sample))
        if distance < NY // 2:
            for step in (distance, NY - distance):
                pair.append((lax.rem(chip_y + step, NY) * NZ + chip_z, sample))
        return pair

    barrier = pltpu.get_barrier_semaphore()
    near = [above, below] + ring_pair(1) + [device for _, device in x_peers]
    for device in near:
        pl.semaphore_signal(barrier, inc=1, device_id=device, device_id_type=MESH)

    def tell(turn):
        for device in ring_pair(2**turn):
            pl.semaphore_signal(ready.at[turn], inc=1, device_id=device, device_id_type=MESH)

    def hear(turn):
        pl.semaphore_wait(ready.at[turn], len(ring_pair(2**turn)))

    loads[0].wait()
    loads[1].wait()
    y_index = lax.broadcasted_iota(jnp.int32, (E, C), 0)
    lane = lax.broadcasted_iota(jnp.int32, (E, E, E * E), 2)
    sub = lax.broadcasted_iota(jnp.int32, (E, E, E * E), 1)
    walls = jnp.broadcast_to(wall_ref[...].astype(F32)[:, None, :], (E, E, E * E))
    walls = jnp.where(lane // E == sub, walls, 0.0).reshape(E * E, E * E).astype(BF16)
    voxel = lax.broadcasted_iota(jnp.int32, (E * E, C), 0)
    wide = field_ref[...].astype(F32)
    for x in range(E):
        pick = (lax.rem(voxel, E) == x).astype(BF16)
        open_x = 1.0 - jnp.dot(walls, pick, preferred_element_type=F32)
        fluid[x] = open_x.reshape(E, E, C)
        column = wide[:, :, x * C : (x + 1) * C]
        field[x] = column
        masked = column * fluid[x]
        conv[x] = masked
        rims[0, x] = masked[E - 2 :].reshape(2 * E, C).astype(BF16)
        rims[1, x] = masked[:2].reshape(2 * E, C).astype(BF16)

    pl.semaphore_wait(barrier, len(near))
    send(rims.at[0], halos.at[0], halo_send.at[0], halo_recv.at[0], above)
    send(rims.at[1], halos.at[1], halo_send.at[1], halo_recv.at[1], below)
    tell(0)

    clear_sides(padded)

    def own_column(x, carry):
        spread_own(padded, x, conv[x], y_index)
        return carry

    lax.fori_loop(0, E, own_column, 0)
    loads[2].wait()

    def spread_weights(pair, carry):
        rows = dw_ref[pair // K, lax.rem(pair, K)]
        weights[pair] = jnp.broadcast_to(rows[:, None, :], (K, E, C))
        return carry

    lax.fori_loop(0, K * K, spread_weights, 0)
    conv_own(padded, weights, conv, False)

    hear(0)
    tell(1)

    for load in loads[3:]:
        load.wait()
    wide = up_ref[...].astype(F32)
    for x in range(E):
        upstream[x] = wide[:, :, x * C : (x + 1) * C]

    layer_index = lax.broadcasted_iota(jnp.int32, (1, layers), 1)

    def position(layer):
        return jnp.sum(jnp.where(layer_index == layer, pos_ref[...], 0), axis=1, keepdims=True)

    own_pos, low_pos, high_pos = position(space), position(space - 1), position(space + 1)
    step_low = (low_pos // 2 - own_pos // 2, low_pos % 2 - own_pos % 2)
    step_high = (high_pos // 2 - own_pos // 2, high_pos % 2 - own_pos % 2)

    def place_halos(dest, received):
        spread_halo(dest, received.at[0], 0, *step_low, space > 0, y_index)
        spread_halo(dest, received.at[1], 2 + E, *step_high, space < layers - 1, y_index)

    for side in range(2):
        wait_bytes(halos.at[side], halo_recv.at[side])
    place_halos(padded, halos)
    conv_halo(padded, weights, conv, False)

    vec_sum[...] = jnp.zeros_like(vec_sum)
    bin_sum[...] = jnp.zeros_like(bin_sum)
    b_in = jnp.concatenate([bin_ref[part : part + 1] for part in range(H // LANES)], axis=1)
    gain, bias, bout, scale = gain_ref[...], bias_ref[...], bout_ref[...], scale_ref[...]
    count = ROWS * E * E

    def by_sublane(values):
        return jnp.sum(values.reshape(count // E, E, values.shape[1]), axis=0)

    def dense(step, carry):
        columns = pl.ds(step * ROWS, ROWS)
        rows = pl.ds(pl.multiple_of(step * count, count), count)
        conv_rows = conv[columns].reshape(count, C)
        row_mean = jnp.mean(conv_rows, axis=1, keepdims=True)
        centred = conv_rows - row_mean
        row_var = jnp.mean(centred * centred, axis=1, keepdims=True)
        inv_std = lax.rsqrt(row_var + NORM_EPS)
        unit_rows = centred * inv_std
        normed = (unit_rows * gain + bias).astype(BF16)
        pre_act = jnp.dot(normed, win_ref[...], preferred_element_type=F32) + b_in
        square = pre_act * pre_act
        tanh_value = jnp.tanh(GELU_SCALE * (pre_act + GELU_CUBIC * square * pre_act))
        half = 0.5 * (1.0 + tanh_value)
        activated = (pre_act * half).astype(BF16)
        slope = half + 0.5 * pre_act * (1.0 - tanh_value * tanh_value) * (
            GELU_SCALE * (1.0 + 3.0 * GELU_CUBIC * square)
        )
        branch = (
            lax.dot_general(
                activated, wout_ref[...], (((1,), (1,)), ((), ())), preferred_element_type=F32
            )
            + bout
        )
        mixed[columns] = (field[columns].reshape(count, C) + scale * branch).reshape(ROWS, E, E, C)
        seed = upstream[columns].reshape(count, C)
        grad_branch = (seed * scale).astype(BF16)
        grad_act = jnp.dot(grad_branch, wout_ref[...], preferred_element_type=F32)
        grad_pre = (grad_act * slope).astype(BF16)
        grad_normed = lax.dot_general(
            grad_pre, win_ref[...], (((1,), (1,)), ((), ())), preferred_element_type=F32
        )
        scaled = grad_normed * gain
        grad_conv = inv_std * (
            scaled
            - jnp.mean(scaled, axis=1, keepdims=True)
            - unit_rows * jnp.mean(scaled * unit_rows, axis=1, keepdims=True)
        )
        grad[columns] = grad_conv.astype(BF16).astype(F32).reshape(ROWS, E, E, C)
        normed_all[rows] = normed
        act_all[rows] = activated
        gpre_all[rows] = grad_pre
        gbranch_all[rows] = grad_branch
        vec_sum[0] += by_sublane(grad_normed * unit_rows)
        vec_sum[1] += by_sublane(grad_normed)
        vec_sum[2] += by_sublane(grad_branch.astype(F32))
        vec_sum[3] += by_sublane(seed * branch)
        bin_sum[...] += by_sublane(grad_pre.astype(F32))
        return carry

    lax.fori_loop(0, E // ROWS, dense, 0)

    def grad_rims(x, carry):
        grims[0, x] = grad[x, E - 2 :].reshape(2 * E, C).astype(BF16)
        grims[1, x] = grad[x, :2].reshape(2 * E, C).astype(BF16)
        return carry

    lax.fori_loop(0, E, grad_rims, 0)
    send(grims.at[0], ghalos.at[0], halo_send.at[2], halo_recv.at[2], above)
    send(grims.at[1], ghalos.at[1], halo_send.at[3], halo_recv.at[3], below)

    by_rows = (((0,), (0,)), ((), ()))
    for base, left, right in ((0, normed_all, gpre_all), (18, gbranch_all, act_all)):
        product = lax.dot_general(left[...], right[...], by_rows, preferred_element_type=F32)
        for part in range(H // LANES):
            piece = product[:, part * LANES : (part + 1) * LANES].astype(BF16)
            w_out1[base + 6 * part : base + 6 * part + 6] = piece.reshape(6, TILE, LANES)
    vec_tile[...] = jnp.zeros_like(vec_tile)
    bin_row = jnp.sum(bin_sum[...], axis=0, keepdims=True)
    for part in range(H // LANES):
        vec_tile[part : part + 1] = bin_row[:, part * LANES : (part + 1) * LANES]
    for row in range(4):
        vec_tile[3 + row : 4 + row, 0:C] = jnp.sum(vec_sum[row], axis=0, keepdims=True)
    w_out1[36] = vec_tile[...].astype(BF16)
    w_out1[37:W_TILES] = jnp.zeros((W_TILES - 37, TILE, LANES), BF16)
    send_all(
        x_peers, lambda peer: w_out1.at[pl.ds(peer * W_SHARE, W_SHARE)],
        lambda slot: w_in1.at[slot], send_sem.at[0], recv_sem.at[0],
    )
    hear(1)
    tell(2)

    kernel_rows[...] = jnp.zeros_like(kernel_rows)

    def kernel_pair(pair, carry):
        tap_z = pair // K
        tap_y = lax.rem(pair, K)
        sums = [jnp.zeros((E, C), F32) for _ in range(K)]
        for z in range(E):
            window = padded[tap_y, :, z + tap_z]
            factor = grad[:, z]
            for tap_x in range(K):
                sums[tap_x] = sums[tap_x] + jnp.sum(window[tap_x : tap_x + E] * factor, axis=0)
        for tap_x in range(K):
            total = jnp.sum(sums[tap_x], axis=0, keepdims=True)
            kernel_rows[pl.ds(pair * K + tap_x, 1), 0:C] = total
        return carry

    lax.fori_loop(0, K * K, kernel_pair, 0)
    k_out1[...] = kernel_rows[...].astype(BF16).reshape(K_TILES, TILE, LANES)
    send_all(
        x_peers, lambda peer: k_out1.at[pl.ds(peer * K_SHARE, K_SHARE)],
        lambda slot: k_in1.at[slot], send_sem.at[5], recv_sem.at[5],
    )

    def own_grad_column(x, carry):
        spread_own(gpadded, x, grad[x], y_index)
        return carry

    lax.fori_loop(0, E, own_grad_column, 0)

    wait_bytes(w_in1, recv_sem.at[0])
    total = add_all(w_out1[pl.ds(sample * W_SHARE, W_SHARE)], w_in1, NS - 1)
    w_out2[0:W_SHARE] = total.astype(BF16)
    if NY * PART > W_SHARE:
        w_out2[W_SHARE : NY * PART] = jnp.zeros((NY * PART - W_SHARE, TILE, LANES), BF16)
    send_all(
        y_peers, lambda peer: w_out2.at[pl.ds(peer * PART, PART)],
        lambda slot: w_in2.at[slot], send_sem.at[1], recv_sem.at[1],
    )

    conv_own(gpadded, weights, conv, True)

    wait_bytes(k_in1, recv_sem.at[5])
    total = add_all(k_out1[pl.ds(sample * K_SHARE, K_SHARE)], k_in1, NS - 1)
    k_out2[...] = total.astype(BF16)
    send_all(
        y_peers, lambda peer: k_out2, lambda slot: k_in2.at[slot], send_sem.at[6], recv_sem.at[6]
    )

    wait_bytes(w_in2, recv_sem.at[1])
    total = add_all(w_out2[pl.ds(chip_y * PART, PART)], w_in2, NY - 1)
    w_out3[...] = total.astype(BF16)
    hear(2)
    send_all(
        z_peers, lambda peer: w_out3, lambda slot: w_in3.at[slot], send_sem.at[2], recv_sem.at[2]
    )

    for side in range(2):
        wait_bytes(ghalos.at[side], halo_recv.at[2 + side])
    place_halos(gpadded, ghalos)

    wait_bytes(k_in2, recv_sem.at[6])
    k_out3[...] = add_all(k_out2[...], k_in2, NY - 1).astype(BF16)
    send_all(
        z_peers, lambda peer: k_out3, lambda slot: k_in3.at[slot], send_sem.at[7], recv_sem.at[7]
    )

    conv_halo(gpadded, weights, conv, True)

    for x in range(E):
        lanes = slice(x * C, (x + 1) * C)
        mixed_ref[:, :, lanes] = mixed[x].astype(BF16)
        gfield_ref[:, :, lanes] = (upstream[x] + conv[x] * fluid[x]).astype(BF16)
    stores[0].start()
    stores[1].start()

    wait_bytes(w_in3, recv_sem.at[2])
    mine = pl.ds(chip_y * PART, PART)
    w_share[mine] = add_all(w_out3[...], w_in3, NZ - 1).astype(BF16)
    send_all(
        y_peers, lambda peer: w_share.at[mine], lambda slot: w_share.at[mine],
        send_sem.at[3], recv_sem.at[3],
    )

    wait_bytes(k_in3, recv_sem.at[7])
    k_all[sample] = add_all(k_out3[...], k_in3, NZ - 1).astype(BF16)
    send_all(
        x_peers, lambda peer: k_all.at[sample], lambda slot: k_all.at[sample],
        send_sem.at[8], recv_sem.at[8],
    )

    wait_bytes(w_share.at[0 : (NY - 1) * PART], recv_sem.at[3])
    w_all[sample] = w_share[0:W_SHARE]
    send_all(
        x_peers, lambda peer: w_all.at[sample], lambda slot: w_all.at[sample],
        send_sem.at[4], recv_sem.at[4],
    )

    wait_bytes(k_all.at[0 : NS - 1], recv_sem.at[8])
    factor = 1.0 / math.sqrt(NS * layers * E**3)

    rows = k_all[...].astype(F32).reshape(K_TILES * TILE, LANES)[:, 0:C] * factor
    for pair in range(K * K):
        gkernel_ref[pair // K, pair % K] = rows[pair * K : (pair + 1) * K]
    stores[2].start()

    wait_bytes(w_all.at[0 : NS - 1], recv_sem.at[4])

    def tile_of(index):
        return w_all[index // W_SHARE, index % W_SHARE].astype(F32) * factor

    for part in range(H // LANES):
        lanes = slice(part * LANES, (part + 1) * LANES)
        for row in range(6):
            gwin_ref[row * TILE : (row + 1) * TILE, lanes] = tile_of(6 * part + row)
            gwout_ref[row * TILE : (row + 1) * TILE, lanes] = tile_of(18 + 6 * part + row)
    last = tile_of(36)
    for part in range(H // LANES):
        gbin_ref[part : part + 1] = last[part : part + 1]
    gvec_ref[...] = last[3:7, 0:C]
    for store in stores[3:]:
        store.start()

    for side in range(2):
        wait_bytes(rims.at[side], halo_send.at[side])
        wait_bytes(grims.at[side], halo_send.at[2 + side])
    sent = (
        w_in1, w_in2, w_in3, w_share.at[0 : (NY - 1) * PART], w_all.at[0 : NS - 1],
        k_in1, k_in2, k_in3, k_all.at[0 : NS - 1],
    )
    for index, ref in enumerate(sent):
        wait_bytes(ref, send_sem.at[index])
    for store in stores:
        store.wait()


def write_out(*refs):
    sources, dests, held, sem = refs[:7], refs[7:14], refs[14:21], refs[21]
    loads = [pltpu.make_async_copy(a, b, sem.at[0, i]) for i, (a, b) in enumerate(zip(sources, held))]
    stores = [pltpu.make_async_copy(a, b, sem.at[1, i]) for i, (a, b) in enumerate(zip(held, dests))]
    for load in loads:
        load.start()
    for load, store in zip(loads, stores):
        load.wait()
        store.start()
    for store in stores:
        store.wait()


def local(
    features, wall_mask, block_positions, dw_kernel, norm_gain, norm_bias, w_in, b_in, w_out, b_out,
    layer_scale, upstream,
):
    voxels = (E, E, E, C)
    spread = (K, E + 4, E + 4, E, C)
    rows = E**3
    hbm = pl.BlockSpec(memory_space=pltpu.HBM)
    outs = (
        jax.ShapeDtypeStruct((E, E, E * C), BF16),
        jax.ShapeDtypeStruct((E, E, E * C), BF16),
        jax.ShapeDtypeStruct((K, K, K, C), F32),
        jax.ShapeDtypeStruct((C, H), F32),
        jax.ShapeDtypeStruct((C, H), F32),
        jax.ShapeDtypeStruct((H // LANES, LANES), F32),
        jax.ShapeDtypeStruct((4, C), F32),
    )
    scratch = [
        pltpu.VMEM((K * K, K, E, C), F32),
        pltpu.VMEM(spread, F32),
        pltpu.VMEM(spread, F32),
        pltpu.VMEM(voxels, F32),
        pltpu.VMEM(voxels, F32),
        pltpu.VMEM(voxels, F32),
        pltpu.VMEM(voxels, F32),
        pltpu.VMEM(voxels, F32),
        pltpu.VMEM(voxels, F32),
        pltpu.VMEM((rows, C), BF16),
        pltpu.VMEM((rows, H), BF16),
        pltpu.VMEM((rows, H), BF16),
        pltpu.VMEM((rows, C), BF16),
        pltpu.VMEM((4, E, C), F32),
        pltpu.VMEM((E, H), F32),
        pltpu.VMEM((K_TILES * TILE, LANES), F32),
        pltpu.VMEM((TILE, LANES), F32),
        pltpu.VMEM((2, E, 2 * E, C), BF16),
        pltpu.VMEM((2, E, 2 * E, C), BF16),
        pltpu.VMEM((2, E, 2 * E, C), BF16),
        pltpu.VMEM((2, E, 2 * E, C), BF16),
        *(pltpu.VMEM((*lead, TILE, LANES), BF16) for lead in (
            (W_TILES,), (NS - 1, W_SHARE), (NY * PART,), (NY - 1, PART), (PART,), (NZ - 1, PART),
            (NY * PART,), (NS, W_SHARE),
            (K_TILES,), (NS - 1, K_SHARE), (K_SHARE,), (NY - 1, K_SHARE), (K_SHARE,),
            (NZ - 1, K_SHARE), (NS, K_SHARE),
        )),
        *(pltpu.VMEM(shape, dtype) for shape, dtype in (
            ((E, E, E * C), BF16), ((E, E * E), jnp.int32), ((1, NY * NZ), jnp.int32),
            ((K, K, K, C), F32), ((1, C), F32), ((1, C), F32), ((C, H), BF16),
            ((H // LANES, LANES), F32), ((C, H), BF16), ((1, C), F32), ((1, C), F32),
            ((E, E, E * C), BF16),
        )),
        *(pltpu.VMEM(out.shape, out.dtype) for out in outs),
        pltpu.SemaphoreType.DMA((4,)),
        pltpu.SemaphoreType.DMA((4,)),
        pltpu.SemaphoreType.DMA((9,)),
        pltpu.SemaphoreType.DMA((9,)),
        pltpu.SemaphoreType.DMA((12,)),
        pltpu.SemaphoreType.DMA((7,)),
        pltpu.SemaphoreType.REGULAR((3,)),
    ]
    results = pl.pallas_call(
        body,
        out_shape=outs,
        in_specs=[hbm] * 12,
        out_specs=[hbm] * 7,
        scratch_shapes=scratch,
        compiler_params=pltpu.CompilerParams(
            collective_id=0, has_side_effects=True, vmem_limit_bytes=VMEM_BYTES
        ),
        cost_estimate=pl.CostEstimate(flops=400_000_000, bytes_accessed=1_500_000, transcendentals=200_000),
        name="block_step",
    )(
        features[0, 0, 0],
        wall_mask[0, 0, 0],
        block_positions[:, :, 0],
        dw_kernel,
        norm_gain[None],
        norm_bias[None],
        w_in,
        b_in.reshape(H // LANES, LANES),
        w_out.T,
        b_out[None],
        layer_scale[None],
        upstream[0, 0, 0],
    )
    results = pl.pallas_call(
        write_out,
        out_shape=outs,
        in_specs=[hbm] * 7,
        out_specs=[hbm] * 7,
        scratch_shapes=[
            *(pltpu.VMEM(out.shape, out.dtype) for out in outs),
            pltpu.SemaphoreType.DMA((2, 7)),
        ],
        compiler_params=pltpu.CompilerParams(vmem_limit_bytes=VMEM_BYTES),
        cost_estimate=pl.CostEstimate(flops=0, bytes_accessed=1_000_000, transcendentals=0),
        name="write_results",
    )(*results)
    mixed, gfield, gkernel, gwin, gwout, gbin, gvec = results
    return (mixed[None, None, None], gfield[None, None, None], gkernel, gwin, gwout.T, gbin.reshape(H), gvec)


def solution(mesh):
    sharded = P("sample", "space", None, None, None, None)
    return jax.shard_map(
        local,
        mesh=mesh,
        in_specs=(
            sharded,
            P("sample", "space", None, None, None),
            P("sample", None, None),
            P(), P(), P(), P(), P(), P(), P(), P(),
            sharded,
        ),
        out_specs=(sharded, sharded, P(), P(), P(), P(), P()),
        check_vma=False,
    )
```

```python
import math

import jax
import jax.numpy as jnp
from jax import lax
from jax.experimental import pallas as pl
from jax.experimental.pallas import tpu as pltpu
from jax.sharding import PartitionSpec as P

F32 = jnp.float32
BF16 = jnp.bfloat16
MESH = pl.DeviceIdType.MESH

GELU_SCALE = 0.7978845608028654
GELU_CUBIC = 0.044715
NORM_EPS = 1e-06

VMEM_BYTES = 62 * 1024 * 1024
E = 8
K = 5
C = 96
H = 384
NZ = 16
NY = 8
NS = 8
TILE = 16
LANES = 128
W_TILES = 40
K_TILES = 8
W_SHARE = W_TILES // NS
K_SHARE = K_TILES // NS
PART = -(-W_SHARE // NY)
PARAM_SCALE = 1.0 / math.sqrt(NS * NY * NZ * E**3)


def wait_bytes(ref, sem):
    pltpu.make_async_copy(ref, ref, sem).wait()


def send(src, dst, send_sem, recv_sem, device):
    pltpu.make_async_remote_copy(
        src_ref=src,
        dst_ref=dst,
        send_sem=send_sem,
        recv_sem=recv_sem,
        device_id=device,
        device_id_type=MESH,
    ).start()


def ring_order(count):
    return sorted(range(1, count), key=lambda step: -min(step, count - step))


def sample_order():
    chips = NS // 2
    steps = [(x, core) for x in range(chips) for core in range(2) if (x, core) != (0, 0)]
    return sorted(steps, key=lambda step: -min(step[0], chips - step[0]))


def send_all(peers, src, dst, send_sem, recv_sem):
    for slot, (index, device) in enumerate(peers):
        send(src(index), dst(slot), send_sem, recv_sem, device)


def add_all(total, parts, count):
    total = total.astype(F32)
    for slot in range(count):
        total = total + parts[slot].astype(F32)
    return total


def axis_region(index):
    return jnp.where(index < 2, -1, jnp.where(index < 2 + E, 0, 1))


def shifted(block, tap):
    return pltpu.roll(block, (2 - tap) % E, 1)


def spread_own(dest, column, block, y_index):
    for tap in range(K):
        keep = (axis_region(y_index + tap) == 0).astype(F32)
        dest[tap, column + 2, 2 : 2 + E] = shifted(block, tap) * keep


def clear_sides(dest):
    dest[:, 0:2, 2 : 2 + E] = jnp.zeros((K, 2, E, E, C), F32)
    dest[:, 2 + E : 4 + E, 2 : 2 + E] = jnp.zeros((K, 2, E, E, C), F32)


def spread_halo(dest, halo, low, step_y, step_x, exists, y_index):
    for tap in range(K):
        keep_y = (axis_region(y_index + tap) == step_y) & exists
        for region in (-1, 0, 1):
            keep = (keep_y & (step_x == region)).astype(F32)
            first, count = {-1: (0, 2), 0: (2, E), 1: (2 + E, 2)}[region]
            source = (first + E - 2) % E
            block = halo[source : source + count].astype(F32).reshape(count * 2, E, C)
            block = shifted(block, tap).reshape(count, 2, E, C) * keep
            dest[tap, first : first + count, low : low + 2] = block


def tap_row(weights, tap_z, tap_y, tap_x, reverse):
    pair = tap_z * K + tap_y
    return weights[K * K - 1 - pair, K - 1 - tap_x] if reverse else weights[pair, tap_x]


def plane_sum(field, weights, total, z, tap_z, reverse):
    for tap_y in range(K):
        window = field[tap_y, :, z + tap_z]
        for tap_x in range(K):
            row = tap_row(weights, tap_z, tap_y, tap_x, reverse)
            total = total + window[tap_x : tap_x + E] * row
    return total


def conv_own(field, weights, out, reverse):
    def tap_layer(tap_z, first):
        def plane(z, carry):
            totals = [None] * E
            for tap_y in range(K):
                window = field[tap_y, 2 : 2 + E, z + tap_z]
                for tap_x in range(K):
                    row = tap_row(weights, tap_z, tap_y, tap_x, reverse)
                    for x in range(max(0, 2 - tap_x), min(E, E + 2 - tap_x)):
                        term = window[x + tap_x - 2] * row
                        totals[x] = term if totals[x] is None else totals[x] + term
            for x in range(E):
                out[x, z] = totals[x] if first else out[x, z] + totals[x]
            return carry

        lax.fori_loop(max(0, 2 - tap_z), min(E, E + 2 - tap_z), plane, 0)

    for tap_z in (2, 0, 1, 3, 4):
        tap_layer(tap_z, tap_z == 2)


def conv_halo(field, weights, out, reverse):
    for z, taps in ((0, (0, 1)), (1, (0,)), (6, (4,)), (7, (3, 4))):
        total = out[:, z]
        for tap_z in taps:
            total = plane_sum(field, weights, total, z, tap_z, reverse)
        out[:, z] = total


def body(
    field_hbm, wall_hbm, pos_hbm, dw_hbm, gain_hbm, bias_hbm, win_hbm, bin_hbm, wout_hbm, bout_hbm,
    scale_hbm, up_hbm,
    mixed_hbm, gfield_hbm, gkernel_hbm, w_hbm,
    weights, padded, gpadded, conv, grad, fluid, field, upstream, mixed,
    normed_all, act_all, gpre_all, gbranch_all, vec_sum, bin_sum, kernel_rows, vec_tile,
    rims, halos, grims, ghalos,
    w_out1, w_in1, w_out2, w_in2, w_out3, w_in3, w_share,
    k_out1, k_in1, k_out2, k_in2, k_out3, k_in3, k_all,
    field_ref, wall_ref, pos_ref, dw_ref, gain_ref, bias_ref, win_ref, bin_ref, wout_ref, bout_ref,
    scale_ref, up_ref,
    mixed_ref, gfield_ref, gkernel_ref,
    halo_send, halo_recv, send_sem, recv_sem, load_sem, store_sem, ready,
):
    stores = [
        pltpu.make_async_copy(source, dest, store_sem.at[index])
        for index, (source, dest) in enumerate((
            (mixed_ref, mixed_hbm), (gfield_ref, gfield_hbm), (gkernel_ref, gkernel_hbm),
        ))
    ]
    loads = [
        pltpu.make_async_copy(source, dest, load_sem.at[index])
        for index, (source, dest) in enumerate((
            (field_hbm, field_ref), (wall_hbm, wall_ref), (dw_hbm, dw_ref), (up_hbm, up_ref),
            (pos_hbm, pos_ref), (gain_hbm, gain_ref), (bias_hbm, bias_ref), (win_hbm, win_ref),
            (bin_hbm, bin_ref), (wout_hbm, wout_ref), (bout_hbm, bout_ref), (scale_hbm, scale_ref),
        ))
    ]
    for load in loads:
        load.start()
    space = lax.axis_index("space")
    sample = lax.axis_index("sample")
    layers = NY * NZ
    chip_y = space // NZ
    chip_z = lax.rem(space, NZ)
    above = (lax.rem(space + 1, layers), sample)
    below = (lax.rem(space + layers - 1, layers), sample)

    x_peers = []
    for step_x, step_core in sample_order():
        x = lax.rem(sample // 2 + step_x, NS // 2)
        index = x * 2 + lax.rem(sample + step_core, 2)
        x_peers.append((index, (space, index)))
    y_peers = []
    for step in ring_order(NY):
        index = lax.rem(chip_y + step, NY)
        y_peers.append((index, (index * NZ + chip_z, sample)))
    z_peers = []
    for step in ring_order(NZ):
        index = lax.rem(chip_z + step, NZ)
        z_peers.append((index, (chip_y * NZ + index, sample)))

    def ring_pair(distance):
        pair = []
        if distance < NZ // 2:
            for step in (distance, NZ - distance):
                pair.append((chip_y * NZ + lax.rem(chip_z + step, NZ), sample))
        if distance < NY // 2:
            for step in (distance, NY - distance):
                pair.append((lax.rem(chip_y + step, NY) * NZ + chip_z, sample))
        return pair

    barrier = pltpu.get_barrier_semaphore()
    near = [above, below] + ring_pair(1) + [device for _, device in x_peers]
    for device in near:
        pl.semaphore_signal(barrier, inc=1, device_id=device, device_id_type=MESH)

    def tell(turn):
        for device in ring_pair(2**turn):
            pl.semaphore_signal(ready.at[turn], inc=1, device_id=device, device_id_type=MESH)

    def hear(turn):
        pl.semaphore_wait(ready.at[turn], len(ring_pair(2**turn)))

    loads[0].wait()
    loads[1].wait()
    y_index = lax.broadcasted_iota(jnp.int32, (E, C), 0)
    lane = lax.broadcasted_iota(jnp.int32, (E, E, E * E), 2)
    sub = lax.broadcasted_iota(jnp.int32, (E, E, E * E), 1)
    walls = jnp.broadcast_to(wall_ref[...].astype(F32)[:, None, :], (E, E, E * E))
    walls = jnp.where(lane // E == sub, walls, 0.0).reshape(E * E, E * E).astype(BF16)
    voxel = lax.broadcasted_iota(jnp.int32, (E * E, C), 0)
    wide = field_ref[...].astype(F32)
    for x in range(E):
        pick = (lax.rem(voxel, E) == x).astype(BF16)
        open_x = 1.0 - jnp.dot(walls, pick, preferred_element_type=F32)
        fluid[x] = open_x.reshape(E, E, C)
        column = wide[:, :, x * C : (x + 1) * C]
        field[x] = column
        masked = column * fluid[x]
        conv[x] = masked
        rims[0, x] = masked[E - 2 :].reshape(2 * E, C).astype(BF16)
        rims[1, x] = masked[:2].reshape(2 * E, C).astype(BF16)

    pl.semaphore_wait(barrier, len(near))
    send(rims.at[0], halos.at[0], halo_send.at[0], halo_recv.at[0], above)
    send(rims.at[1], halos.at[1], halo_send.at[1], halo_recv.at[1], below)
    tell(0)

    clear_sides(padded)

    def own_column(x, carry):
        spread_own(padded, x, conv[x], y_index)
        return carry

    lax.fori_loop(0, E, own_column, 0)
    loads[2].wait()

    def spread_weights(pair, carry):
        rows = dw_ref[pair // K, lax.rem(pair, K)]
        weights[pair] = jnp.broadcast_to(rows[:, None, :], (K, E, C))
        return carry

    lax.fori_loop(0, K * K, spread_weights, 0)
    conv_own(padded, weights, conv, False)

    hear(0)
    tell(1)

    for load in loads[3:]:
        load.wait()
    wide = up_ref[...].astype(F32)
    for x in range(E):
        upstream[x] = wide[:, :, x * C : (x + 1) * C]

    layer_index = lax.broadcasted_iota(jnp.int32, (1, layers), 1)

    def position(layer):
        return jnp.sum(jnp.where(layer_index == layer, pos_ref[...], 0), axis=1, keepdims=True)

    own_pos, low_pos, high_pos = position(space), position(space - 1), position(space + 1)
    step_low = (low_pos // 2 - own_pos // 2, low_pos % 2 - own_pos % 2)
    step_high = (high_pos // 2 - own_pos // 2, high_pos % 2 - own_pos % 2)

    def place_halos(dest, received):
        spread_halo(dest, received.at[0], 0, *step_low, space > 0, y_index)
        spread_halo(dest, received.at[1], 2 + E, *step_high, space < layers - 1, y_index)

    for side in range(2):
        wait_bytes(halos.at[side], halo_recv.at[side])
    place_halos(padded, halos)
    conv_halo(padded, weights, conv, False)

    b_in = jnp.concatenate([bin_ref[part : part + 1] for part in range(H // LANES)], axis=1)
    gain, bias, bout, scale = gain_ref[...], bias_ref[...], bout_ref[...], scale_ref[...]
    count = E * E * E

    def by_sublane(values):
        return jnp.sum(values.reshape(count // E, E, values.shape[1]), axis=0)

    conv_rows = conv[...].reshape(count, C)
    row_mean = jnp.mean(conv_rows, axis=1, keepdims=True)
    centred = conv_rows - row_mean
    row_var = jnp.mean(centred * centred, axis=1, keepdims=True)
    inv_std = lax.rsqrt(row_var + NORM_EPS)
    unit_rows = centred * inv_std
    normed = (unit_rows * gain + bias).astype(BF16)
    pre_act = jnp.dot(normed, win_ref[...], preferred_element_type=F32) + b_in
    square = pre_act * pre_act
    tanh_value = jnp.tanh(GELU_SCALE * (pre_act + GELU_CUBIC * square * pre_act))
    half = 0.5 * (1.0 + tanh_value)
    activated = (pre_act * half).astype(BF16)
    slope = half + 0.5 * pre_act * (1.0 - tanh_value * tanh_value) * (
        GELU_SCALE * (1.0 + 3.0 * GELU_CUBIC * square)
    )
    branch = (
        lax.dot_general(
            activated, wout_ref[...], (((1,), (1,)), ((), ())), preferred_element_type=F32
        )
        + bout
    )
    mixed[...] = (field[...].reshape(count, C) + scale * branch).reshape(E, E, E, C)
    seed = upstream[...].reshape(count, C)
    grad_branch = (seed * scale).astype(BF16)
    grad_act = jnp.dot(grad_branch, wout_ref[...], preferred_element_type=F32)
    grad_pre = (grad_act * slope).astype(BF16)
    grad_normed = lax.dot_general(
        grad_pre, win_ref[...], (((1,), (1,)), ((), ())), preferred_element_type=F32
    )
    normed_all[...] = normed
    act_all[...] = activated
    gpre_all[...] = grad_pre
    gbranch_all[...] = grad_branch
    vec_sum[0] = by_sublane(grad_normed * unit_rows)
    vec_sum[1] = by_sublane(grad_normed)
    vec_sum[2] = by_sublane(grad_branch.astype(F32))
    vec_sum[3] = by_sublane(seed * branch)
    bin_sum[...] = by_sublane(grad_pre.astype(F32))
    by_rows = (((0,), (0,)), ((), ()))
    for base, left, right in ((0, normed_all, gpre_all), (18, gbranch_all, act_all)):
        product = lax.dot_general(left[...], right[...], by_rows, preferred_element_type=F32)
        for part in range(H // LANES):
            piece = product[:, part * LANES : (part + 1) * LANES].astype(BF16)
            w_out1[base + 6 * part : base + 6 * part + 6] = piece.reshape(6, TILE, LANES)
    vec_tile[...] = jnp.zeros_like(vec_tile)
    bin_row = jnp.sum(bin_sum[...], axis=0, keepdims=True)
    for part in range(H // LANES):
        vec_tile[part : part + 1] = bin_row[:, part * LANES : (part + 1) * LANES]
    for row in range(4):
        vec_tile[3 + row : 4 + row, 0:C] = jnp.sum(vec_sum[row], axis=0, keepdims=True)
    w_out1[36] = vec_tile[...].astype(BF16)
    w_out1[37:W_TILES] = jnp.zeros((W_TILES - 37, TILE, LANES), BF16)
    send_all(
        x_peers, lambda peer: w_out1.at[pl.ds(peer * W_SHARE, W_SHARE)],
        lambda slot: w_in1.at[slot], send_sem.at[0], recv_sem.at[0],
    )
    hear(1)
    tell(2)

    scaled = grad_normed * gain
    grad_conv = inv_std * (
        scaled
        - jnp.mean(scaled, axis=1, keepdims=True)
        - unit_rows * jnp.mean(scaled * unit_rows, axis=1, keepdims=True)
    )
    grad[...] = grad_conv.astype(BF16).astype(F32).reshape(E, E, E, C)

    def grad_rims(x, carry):
        grims[0, x] = grad[x, E - 2 :].reshape(2 * E, C).astype(BF16)
        grims[1, x] = grad[x, :2].reshape(2 * E, C).astype(BF16)
        return carry

    lax.fori_loop(0, E, grad_rims, 0)
    send(grims.at[0], ghalos.at[0], halo_send.at[2], halo_recv.at[2], above)
    send(grims.at[1], ghalos.at[1], halo_send.at[3], halo_recv.at[3], below)


    kernel_rows[...] = jnp.zeros_like(kernel_rows)

    def kernel_layer(tap_z):
        def kernel_pair(tap_y, carry):
            sums = [jnp.zeros((E, C), F32) for _ in range(K)]
            for z in range(E):
                window = padded[tap_y, :, z + tap_z]
                factor = grad[:, z]
                own = 2 <= z + tap_z < 2 + E
                for tap_x in range(K):
                    low, high = (max(0, 2 - tap_x), min(E, E + 2 - tap_x)) if own else (0, E)
                    product = window[low + tap_x : high + tap_x] * factor[low:high]
                    sums[tap_x] = sums[tap_x] + jnp.sum(product, axis=0)
            for tap_x in range(K):
                total = jnp.sum(sums[tap_x], axis=0, keepdims=True)
                kernel_rows[pl.ds((tap_z * K + tap_y) * K + tap_x, 1), 0:C] = total
            return carry

        lax.fori_loop(0, K, kernel_pair, 0)

    for tap_z in range(K):
        kernel_layer(tap_z)
    k_out1[...] = kernel_rows[...].astype(BF16).reshape(K_TILES, TILE, LANES)
    send_all(
        x_peers, lambda peer: k_out1.at[pl.ds(peer * K_SHARE, K_SHARE)],
        lambda slot: k_in1.at[slot], send_sem.at[5], recv_sem.at[5],
    )

    wait_bytes(w_in1, recv_sem.at[0])
    total = add_all(w_out1[pl.ds(sample * W_SHARE, W_SHARE)], w_in1, NS - 1)
    w_out2[0:W_SHARE] = total.astype(BF16)
    if NY * PART > W_SHARE:
        w_out2[W_SHARE : NY * PART] = jnp.zeros((NY * PART - W_SHARE, TILE, LANES), BF16)
    send_all(
        y_peers, lambda peer: w_out2.at[pl.ds(peer * PART, PART)],
        lambda slot: w_in2.at[slot], send_sem.at[1], recv_sem.at[1],
    )

    def own_grad_column(x, carry):
        spread_own(gpadded, x, grad[x], y_index)
        return carry

    lax.fori_loop(0, E, own_grad_column, 0)

    conv_own(gpadded, weights, conv, True)

    wait_bytes(k_in1, recv_sem.at[5])
    total = add_all(k_out1[pl.ds(sample * K_SHARE, K_SHARE)], k_in1, NS - 1)
    k_out2[...] = total.astype(BF16)
    send_all(
        y_peers, lambda peer: k_out2, lambda slot: k_in2.at[slot], send_sem.at[6], recv_sem.at[6]
    )

    wait_bytes(w_in2, recv_sem.at[1])
    total = add_all(w_out2[pl.ds(chip_y * PART, PART)], w_in2, NY - 1)
    w_out3[...] = total.astype(BF16)
    hear(2)
    send_all(
        z_peers, lambda peer: w_out3, lambda slot: w_in3.at[slot], send_sem.at[2], recv_sem.at[2]
    )

    for side in range(2):
        wait_bytes(ghalos.at[side], halo_recv.at[2 + side])
    place_halos(gpadded, ghalos)

    wait_bytes(k_in2, recv_sem.at[6])
    k_out3[...] = add_all(k_out2[...], k_in2, NY - 1).astype(BF16)
    send_all(
        z_peers, lambda peer: k_out3, lambda slot: k_in3.at[slot], send_sem.at[7], recv_sem.at[7]
    )

    conv_halo(gpadded, weights, conv, True)

    for x in range(E):
        lanes = slice(x * C, (x + 1) * C)
        mixed_ref[:, :, lanes] = mixed[x].astype(BF16)
        gfield_ref[:, :, lanes] = (upstream[x] + conv[x] * fluid[x]).astype(BF16)
    stores[0].start()
    stores[1].start()

    wait_bytes(w_in3, recv_sem.at[2])
    mine = pl.ds(chip_y * PART, PART)
    w_share[mine] = add_all(w_out3[...], w_in3, NZ - 1).astype(BF16)
    send_all(
        y_peers, lambda peer: w_share.at[mine], lambda slot: w_share.at[mine],
        send_sem.at[3], recv_sem.at[3],
    )

    wait_bytes(k_in3, recv_sem.at[7])
    k_all[sample] = add_all(k_out3[...], k_in3, NZ - 1).astype(BF16)
    send_all(
        x_peers, lambda peer: k_all.at[sample], lambda slot: k_all.at[sample],
        send_sem.at[8], recv_sem.at[8],
    )

    wait_bytes(w_share.at[0 : (NY - 1) * PART], recv_sem.at[3])
    mine = w_hbm.at[pl.ds(sample * W_SHARE, W_SHARE)]
    send_all(
        x_peers, lambda peer: w_share.at[0:W_SHARE], lambda slot: mine,
        send_sem.at[4], recv_sem.at[4],
    )
    keep = pltpu.make_async_copy(w_share.at[0:W_SHARE], mine, store_sem.at[3])
    keep.start()

    wait_bytes(k_all.at[0 : NS - 1], recv_sem.at[8])
    rows = k_all[...].astype(F32).reshape(K_TILES * TILE, LANES)[:, 0:C] * PARAM_SCALE
    for pair in range(K * K):
        gkernel_ref[pair // K, pair % K] = rows[pair * K : (pair + 1) * K]
    stores[2].start()

    for side in range(2):
        wait_bytes(rims.at[side], halo_send.at[side])
        wait_bytes(grims.at[side], halo_send.at[2 + side])
    sent = (
        w_in1, w_in2, w_in3, w_share.at[0 : (NY - 1) * PART], w_hbm.at[0 : (NS - 1) * W_SHARE],
        k_in1, k_in2, k_in3, k_all.at[0 : NS - 1],
    )
    for index, ref in enumerate(sent):
        wait_bytes(ref, send_sem.at[index])
    for store in stores:
        store.wait()
    keep.wait()
    wait_bytes(w_hbm.at[0 : (NS - 1) * W_SHARE], recv_sem.at[4])


def write_out(
    mixed_in, gfield_in, gkernel_in, tiles_in,
    mixed_out, gfield_out, gkernel_out, gwin_out, gwout_out, gbin_out, gvec_out,
    mixed, gfield, gkernel, gwin, gwout, gbin, gvec, tiles, sem,
):
    def copies(pairs, first):
        return [pltpu.make_async_copy(a, b, sem.at[first + i]) for i, (a, b) in enumerate(pairs)]

    load_tiles, = copies([(tiles_in, tiles)], 0)
    loads = copies([(mixed_in, mixed), (gfield_in, gfield), (gkernel_in, gkernel)], 1)
    passed = copies([(mixed, mixed_out), (gfield, gfield_out), (gkernel, gkernel_out)], 4)
    made = copies([(gwin, gwin_out), (gwout, gwout_out), (gbin, gbin_out), (gvec, gvec_out)], 7)
    load_tiles.start()
    for load in loads:
        load.start()
    load_tiles.wait()
    for base, dest in ((0, gwin), (18, gwout)):
        for part in range(H // LANES):
            block = tiles[base + 6 * part : base + 6 * part + 6].astype(F32) * PARAM_SCALE
            dest[:, part * LANES : (part + 1) * LANES] = block.reshape(C, LANES)
    last = tiles[36].astype(F32) * PARAM_SCALE
    gbin[...] = last[0:3]
    gvec[...] = last[3:7, 0:C]
    for copy in made:
        copy.start()
    for load, copy in zip(loads, passed):
        load.wait()
        copy.start()
    for copy in passed + made:
        copy.wait()


def local(
    features, wall_mask, block_positions, dw_kernel, norm_gain, norm_bias, w_in, b_in, w_out, b_out,
    layer_scale, upstream,
):
    voxels = (E, E, E, C)
    spread = (K, E + 4, E + 4, E, C)
    rows = E**3
    hbm = pl.BlockSpec(memory_space=pltpu.HBM)
    outs = (
        jax.ShapeDtypeStruct((E, E, E * C), BF16),
        jax.ShapeDtypeStruct((E, E, E * C), BF16),
        jax.ShapeDtypeStruct((K, K, K, C), F32),
        jax.ShapeDtypeStruct((C, H), F32),
        jax.ShapeDtypeStruct((C, H), F32),
        jax.ShapeDtypeStruct((H // LANES, LANES), F32),
        jax.ShapeDtypeStruct((4, C), F32),
    )
    scratch = [
        pltpu.VMEM((K * K, K, E, C), F32),
        pltpu.VMEM(spread, F32),
        pltpu.VMEM(spread, F32),
        pltpu.VMEM(voxels, F32),
        pltpu.VMEM(voxels, F32),
        pltpu.VMEM(voxels, F32),
        pltpu.VMEM(voxels, F32),
        pltpu.VMEM(voxels, F32),
        pltpu.VMEM(voxels, F32),
        pltpu.VMEM((rows, C), BF16),
        pltpu.VMEM((rows, H), BF16),
        pltpu.VMEM((rows, H), BF16),
        pltpu.VMEM((rows, C), BF16),
        pltpu.VMEM((4, E, C), F32),
        pltpu.VMEM((E, H), F32),
        pltpu.VMEM((K_TILES * TILE, LANES), F32),
        pltpu.VMEM((TILE, LANES), F32),
        pltpu.VMEM((2, E, 2 * E, C), BF16),
        pltpu.VMEM((2, E, 2 * E, C), BF16),
        pltpu.VMEM((2, E, 2 * E, C), BF16),
        pltpu.VMEM((2, E, 2 * E, C), BF16),
        *(pltpu.VMEM((*lead, TILE, LANES), BF16) for lead in (
            (W_TILES,), (NS - 1, W_SHARE), (NY * PART,), (NY - 1, PART), (PART,), (NZ - 1, PART),
            (NY * PART,),
            (K_TILES,), (NS - 1, K_SHARE), (K_SHARE,), (NY - 1, K_SHARE), (K_SHARE,),
            (NZ - 1, K_SHARE), (NS, K_SHARE),
        )),
        *(pltpu.VMEM(shape, dtype) for shape, dtype in (
            ((E, E, E * C), BF16), ((E, E * E), jnp.int32), ((1, NY * NZ), jnp.int32),
            ((K, K, K, C), F32), ((1, C), F32), ((1, C), F32), ((C, H), BF16),
            ((H // LANES, LANES), F32), ((C, H), BF16), ((1, C), F32), ((1, C), F32),
            ((E, E, E * C), BF16),
        )),
        *(pltpu.VMEM(out.shape, out.dtype) for out in outs[:3]),
        pltpu.SemaphoreType.DMA((4,)),
        pltpu.SemaphoreType.DMA((4,)),
        pltpu.SemaphoreType.DMA((9,)),
        pltpu.SemaphoreType.DMA((9,)),
        pltpu.SemaphoreType.DMA((12,)),
        pltpu.SemaphoreType.DMA((4,)),
        pltpu.SemaphoreType.REGULAR((3,)),
    ]
    results = pl.pallas_call(
        body,
        out_shape=outs[:3] + (jax.ShapeDtypeStruct((W_TILES, TILE, LANES), BF16),),
        in_specs=[hbm] * 12,
        out_specs=[hbm] * 4,
        scratch_shapes=scratch,
        compiler_params=pltpu.CompilerParams(
            collective_id=0, has_side_effects=True, vmem_limit_bytes=VMEM_BYTES
        ),
        cost_estimate=pl.CostEstimate(flops=400_000_000, bytes_accessed=1_500_000, transcendentals=200_000),
        name="block_step",
    )(
        features[0, 0, 0],
        wall_mask[0, 0, 0],
        block_positions[:, :, 0],
        dw_kernel,
        norm_gain[None],
        norm_bias[None],
        w_in,
        b_in.reshape(H // LANES, LANES),
        w_out.T,
        b_out[None],
        layer_scale[None],
        upstream[0, 0, 0],
    )
    results = pl.pallas_call(
        write_out,
        out_shape=outs,
        in_specs=[hbm] * 4,
        out_specs=[hbm] * 7,
        scratch_shapes=[
            *(pltpu.VMEM(out.shape, out.dtype) for out in outs),
            pltpu.VMEM((W_TILES, TILE, LANES), BF16),
            pltpu.SemaphoreType.DMA((11,)),
        ],
        compiler_params=pltpu.CompilerParams(vmem_limit_bytes=VMEM_BYTES),
        cost_estimate=pl.CostEstimate(flops=0, bytes_accessed=1_000_000, transcendentals=0),
        name="write_results",
    )(*results)
    mixed, gfield, gkernel, gwin, gwout, gbin, gvec = results
    return (mixed[None, None, None], gfield[None, None, None], gkernel, gwin, gwout.T, gbin.reshape(H), gvec)


def solution(mesh):
    sharded = P("sample", "space", None, None, None, None)
    return jax.shard_map(
        local,
        mesh=mesh,
        in_specs=(
            sharded,
            P("sample", "space", None, None, None),
            P("sample", None, None),
            P(), P(), P(), P(), P(), P(), P(), P(),
            sharded,
        ),
        out_specs=(sharded, sharded, P(), P(), P(), P(), P()),
        check_vma=False,
    )
```

```python
import math

import jax
import jax.numpy as jnp
from jax import lax
from jax.experimental import pallas as pl
from jax.experimental.pallas import tpu as pltpu
from jax.sharding import PartitionSpec as P

F32 = jnp.float32
BF16 = jnp.bfloat16
MESH = pl.DeviceIdType.MESH

GELU_SCALE = 0.7978845608028654
GELU_CUBIC = 0.044715
NORM_EPS = 1e-06

VMEM_BYTES = 62 * 1024 * 1024
E = 8
K = 5
C = 96
H = 384
NZ = 16
NY = 8
NS = 8
TILE = 16
LANES = 128
W_TILES = 40
K_TILES = 8
W_SHARE = W_TILES // NS
K_SHARE = K_TILES // NS
PART = -(-W_SHARE // NY)
PARAM_SCALE = 1.0 / math.sqrt(NS * NY * NZ * E**3)


def wait_bytes(ref, sem):
    pltpu.make_async_copy(ref, ref, sem).wait()


def send(src, dst, send_sem, recv_sem, device):
    pltpu.make_async_remote_copy(
        src_ref=src,
        dst_ref=dst,
        send_sem=send_sem,
        recv_sem=recv_sem,
        device_id=device,
        device_id_type=MESH,
    ).start()


def ring_order(count):
    return sorted(range(1, count), key=lambda step: -min(step, count - step))


def sample_order():
    chips = NS // 2
    steps = [(x, core) for x in range(chips) for core in range(2) if (x, core) != (0, 0)]
    return sorted(steps, key=lambda step: -min(step[0], chips - step[0]))


def send_all(peers, src, dst, send_sem, recv_sem):
    for slot, (index, device) in enumerate(peers):
        send(src(index), dst(slot), send_sem, recv_sem, device)


def add_all(total, parts, count):
    total = total.astype(F32)
    for slot in range(count):
        total = total + parts[slot].astype(F32)
    return total


def axis_region(index):
    return jnp.where(index < 2, -1, jnp.where(index < 2 + E, 0, 1))


def shifted(block, tap):
    return pltpu.roll(block, (2 - tap) % E, 1)


def spread_own(dest, column, block, y_index):
    for tap in range(K):
        keep = (axis_region(y_index + tap) == 0).astype(F32)
        dest[tap, column + 2, 2 : 2 + E] = shifted(block, tap) * keep


def clear_sides(dest):
    dest[:, 0:2, 2 : 2 + E] = jnp.zeros((K, 2, E, E, C), F32)
    dest[:, 2 + E : 4 + E, 2 : 2 + E] = jnp.zeros((K, 2, E, E, C), F32)


def spread_halo(dest, halo, low, step_y, step_x, exists, y_index):
    for tap in range(K):
        keep_y = (axis_region(y_index + tap) == step_y) & exists
        for region in (-1, 0, 1):
            keep = (keep_y & (step_x == region)).astype(F32)
            first, count = {-1: (0, 2), 0: (2, E), 1: (2 + E, 2)}[region]
            source = (first + E - 2) % E
            block = halo[source : source + count].astype(F32).reshape(count * 2, E, C)
            block = shifted(block, tap).reshape(count, 2, E, C) * keep
            dest[tap, first : first + count, low : low + 2] = block


def tap_row(weights, tap_z, tap_y, tap_x, reverse):
    pair = tap_z * K + tap_y
    return weights[K * K - 1 - pair, K - 1 - tap_x] if reverse else weights[pair, tap_x]


def plane_sum(field, weights, total, z, tap_z, reverse):
    for tap_y in range(K):
        window = field[tap_y, :, z + tap_z]
        for tap_x in range(K):
            row = tap_row(weights, tap_z, tap_y, tap_x, reverse)
            total = total + window[tap_x : tap_x + E] * row
    return total


def conv_own(field, weights, out, reverse):
    def tap_layer(tap_z, first):
        def plane(z, carry):
            totals = [None] * E
            for tap_y in range(K):
                window = field[tap_y, 2 : 2 + E, z + tap_z]
                for tap_x in range(K):
                    row = tap_row(weights, tap_z, tap_y, tap_x, reverse)
                    for x in range(max(0, 2 - tap_x), min(E, E + 2 - tap_x)):
                        term = window[x + tap_x - 2] * row
                        totals[x] = term if totals[x] is None else totals[x] + term
            for x in range(E):
                out[x, z] = totals[x] if first else out[x, z] + totals[x]
            return carry

        lax.fori_loop(max(0, 2 - tap_z), min(E, E + 2 - tap_z), plane, 0)

    for tap_z in (2, 0, 1, 3, 4):
        tap_layer(tap_z, tap_z == 2)


def conv_halo(field, weights, out, reverse):
    for z, taps in ((0, (0, 1)), (1, (0,)), (6, (4,)), (7, (3, 4))):
        total = out[:, z]
        for tap_z in taps:
            total = plane_sum(field, weights, total, z, tap_z, reverse)
        out[:, z] = total


def body(
    field_hbm, wall_hbm, pos_hbm, dw_hbm, gain_hbm, bias_hbm, win_hbm, bin_hbm, wout_hbm, bout_hbm,
    scale_hbm, up_hbm,
    mixed_hbm, gfield_hbm, k_hbm, w_hbm,
    weights, padded, gpadded, conv, grad, fluid, field, upstream, mixed,
    normed_all, act_all, gpre_all, gbranch_all, vec_sum, bin_sum, kernel_rows, vec_tile,
    rims, halos, grims, ghalos,
    w_out1, w_in1, w_out2, w_in2, w_out3, w_in3, w_share,
    k_out1, k_in1, k_out2, k_in2, k_out3, k_in3, k_share,
    field_ref, wall_ref, pos_ref, dw_ref, gain_ref, bias_ref, win_ref, bin_ref, wout_ref, bout_ref,
    scale_ref, up_ref,
    mixed_ref, gfield_ref,
    halo_send, halo_recv, send_sem, recv_sem, load_sem, store_sem, ready,
):
    stores = [
        pltpu.make_async_copy(source, dest, store_sem.at[index])
        for index, (source, dest) in enumerate((
            (mixed_ref, mixed_hbm), (gfield_ref, gfield_hbm),
        ))
    ]
    loads = [
        pltpu.make_async_copy(source, dest, load_sem.at[index])
        for index, (source, dest) in enumerate((
            (field_hbm, field_ref), (wall_hbm, wall_ref), (dw_hbm, dw_ref), (up_hbm, up_ref),
            (pos_hbm, pos_ref), (gain_hbm, gain_ref), (bias_hbm, bias_ref), (win_hbm, win_ref),
            (bin_hbm, bin_ref), (wout_hbm, wout_ref), (bout_hbm, bout_ref), (scale_hbm, scale_ref),
        ))
    ]
    for load in loads:
        load.start()
    space = lax.axis_index("space")
    sample = lax.axis_index("sample")
    layers = NY * NZ
    chip_y = space // NZ
    chip_z = lax.rem(space, NZ)
    above = (lax.rem(space + 1, layers), sample)
    below = (lax.rem(space + layers - 1, layers), sample)

    x_peers = []
    for step_x, step_core in sample_order():
        x = lax.rem(sample // 2 + step_x, NS // 2)
        index = x * 2 + lax.rem(sample + step_core, 2)
        x_peers.append((index, (space, index)))
    y_peers = []
    for step in ring_order(NY):
        index = lax.rem(chip_y + step, NY)
        y_peers.append((index, (index * NZ + chip_z, sample)))
    z_peers = []
    for step in ring_order(NZ):
        index = lax.rem(chip_z + step, NZ)
        z_peers.append((index, (chip_y * NZ + index, sample)))

    def ring_pair(distance):
        pair = []
        if distance < NZ // 2:
            for step in (distance, NZ - distance):
                pair.append((chip_y * NZ + lax.rem(chip_z + step, NZ), sample))
        if distance < NY // 2:
            for step in (distance, NY - distance):
                pair.append((lax.rem(chip_y + step, NY) * NZ + chip_z, sample))
        return pair

    barrier = pltpu.get_barrier_semaphore()
    near = [above, below] + ring_pair(1) + [device for _, device in x_peers]
    for device in near:
        pl.semaphore_signal(barrier, inc=1, device_id=device, device_id_type=MESH)

    def tell(turn):
        for device in ring_pair(2**turn):
            pl.semaphore_signal(ready.at[turn], inc=1, device_id=device, device_id_type=MESH)

    def hear(turn):
        pl.semaphore_wait(ready.at[turn], len(ring_pair(2**turn)))

    loads[0].wait()
    loads[1].wait()
    y_index = lax.broadcasted_iota(jnp.int32, (E, C), 0)
    lane = lax.broadcasted_iota(jnp.int32, (E, E, E * E), 2)
    sub = lax.broadcasted_iota(jnp.int32, (E, E, E * E), 1)
    walls = jnp.broadcast_to(wall_ref[...].astype(F32)[:, None, :], (E, E, E * E))
    walls = jnp.where(lane // E == sub, walls, 0.0).reshape(E * E, E * E).astype(BF16)
    voxel = lax.broadcasted_iota(jnp.int32, (E * E, C), 0)
    wide = field_ref[...].astype(F32)
    for x in range(E):
        pick = (lax.rem(voxel, E) == x).astype(BF16)
        open_x = 1.0 - jnp.dot(walls, pick, preferred_element_type=F32)
        fluid[x] = open_x.reshape(E, E, C)
        column = wide[:, :, x * C : (x + 1) * C]
        field[x] = column
        masked = column * fluid[x]
        conv[x] = masked
        rims[0, x] = masked[E - 2 :].reshape(2 * E, C).astype(BF16)
        rims[1, x] = masked[:2].reshape(2 * E, C).astype(BF16)

    pl.semaphore_wait(barrier, len(near))
    send(rims.at[0], halos.at[0], halo_send.at[0], halo_recv.at[0], above)
    send(rims.at[1], halos.at[1], halo_send.at[1], halo_recv.at[1], below)
    tell(0)

    clear_sides(padded)

    def own_column(x, carry):
        spread_own(padded, x, conv[x], y_index)
        return carry

    lax.fori_loop(0, E, own_column, 0)
    loads[2].wait()

    def spread_weights(pair, carry):
        rows = dw_ref[pair // K, lax.rem(pair, K)]
        weights[pair] = jnp.broadcast_to(rows[:, None, :], (K, E, C))
        return carry

    lax.fori_loop(0, K * K, spread_weights, 0)
    conv_own(padded, weights, conv, False)

    hear(0)
    tell(1)

    for load in loads[3:]:
        load.wait()
    wide = up_ref[...].astype(F32)
    for x in range(E):
        upstream[x] = wide[:, :, x * C : (x + 1) * C]

    layer_index = lax.broadcasted_iota(jnp.int32, (1, layers), 1)

    def position(layer):
        return jnp.sum(jnp.where(layer_index == layer, pos_ref[...], 0), axis=1, keepdims=True)

    own_pos, low_pos, high_pos = position(space), position(space - 1), position(space + 1)
    step_low = (low_pos // 2 - own_pos // 2, low_pos % 2 - own_pos % 2)
    step_high = (high_pos // 2 - own_pos // 2, high_pos % 2 - own_pos % 2)

    def place_halos(dest, received):
        spread_halo(dest, received.at[0], 0, *step_low, space > 0, y_index)
        spread_halo(dest, received.at[1], 2 + E, *step_high, space < layers - 1, y_index)

    for side in range(2):
        wait_bytes(halos.at[side], halo_recv.at[side])
    place_halos(padded, halos)
    conv_halo(padded, weights, conv, False)

    b_in = jnp.concatenate([bin_ref[part : part + 1] for part in range(H // LANES)], axis=1)
    gain, bias, bout, scale = gain_ref[...], bias_ref[...], bout_ref[...], scale_ref[...]
    count = E * E * E

    def by_sublane(values):
        return jnp.sum(values.reshape(count // E, E, values.shape[1]), axis=0)

    conv_rows = conv[...].reshape(count, C)
    row_mean = jnp.mean(conv_rows, axis=1, keepdims=True)
    centred = conv_rows - row_mean
    row_var = jnp.mean(centred * centred, axis=1, keepdims=True)
    inv_std = lax.rsqrt(row_var + NORM_EPS)
    unit_rows = centred * inv_std
    normed = (unit_rows * gain + bias).astype(BF16)
    pre_act = jnp.dot(normed, win_ref[...], preferred_element_type=F32) + b_in
    square = pre_act * pre_act
    tanh_value = jnp.tanh(GELU_SCALE * (pre_act + GELU_CUBIC * square * pre_act))
    half = 0.5 * (1.0 + tanh_value)
    activated = (pre_act * half).astype(BF16)
    slope = half + 0.5 * pre_act * (1.0 - tanh_value * tanh_value) * (
        GELU_SCALE * (1.0 + 3.0 * GELU_CUBIC * square)
    )
    branch = (
        lax.dot_general(
            activated, wout_ref[...], (((1,), (1,)), ((), ())), preferred_element_type=F32
        )
        + bout
    )
    mixed[...] = (field[...].reshape(count, C) + scale * branch).reshape(E, E, E, C)
    seed = upstream[...].reshape(count, C)
    grad_branch = (seed * scale).astype(BF16)
    grad_act = jnp.dot(grad_branch, wout_ref[...], preferred_element_type=F32)
    grad_pre = (grad_act * slope).astype(BF16)
    grad_normed = lax.dot_general(
        grad_pre, win_ref[...], (((1,), (1,)), ((), ())), preferred_element_type=F32
    )
    normed_all[...] = normed
    act_all[...] = activated
    gpre_all[...] = grad_pre
    gbranch_all[...] = grad_branch
    vec_sum[0] = by_sublane(grad_normed * unit_rows)
    vec_sum[1] = by_sublane(grad_normed)
    vec_sum[2] = by_sublane(grad_branch.astype(F32))
    vec_sum[3] = by_sublane(seed * branch)
    bin_sum[...] = by_sublane(grad_pre.astype(F32))
    by_rows = (((0,), (0,)), ((), ()))
    for base, left, right in ((0, normed_all, gpre_all), (18, gbranch_all, act_all)):
        product = lax.dot_general(left[...], right[...], by_rows, preferred_element_type=F32)
        for part in range(H // LANES):
            piece = product[:, part * LANES : (part + 1) * LANES].astype(BF16)
            w_out1[base + 6 * part : base + 6 * part + 6] = piece.reshape(6, TILE, LANES)
    vec_tile[...] = jnp.zeros_like(vec_tile)
    bin_row = jnp.sum(bin_sum[...], axis=0, keepdims=True)
    for part in range(H // LANES):
        vec_tile[part : part + 1] = bin_row[:, part * LANES : (part + 1) * LANES]
    for row in range(4):
        vec_tile[3 + row : 4 + row, 0:C] = jnp.sum(vec_sum[row], axis=0, keepdims=True)
    w_out1[36] = vec_tile[...].astype(BF16)
    w_out1[37:W_TILES] = jnp.zeros((W_TILES - 37, TILE, LANES), BF16)
    send_all(
        x_peers, lambda peer: w_out1.at[pl.ds(peer * W_SHARE, W_SHARE)],
        lambda slot: w_in1.at[slot], send_sem.at[0], recv_sem.at[0],
    )
    hear(1)
    tell(2)

    scaled = grad_normed * gain
    grad_conv = inv_std * (
        scaled
        - jnp.mean(scaled, axis=1, keepdims=True)
        - unit_rows * jnp.mean(scaled * unit_rows, axis=1, keepdims=True)
    )
    grad[...] = grad_conv.astype(BF16).astype(F32).reshape(E, E, E, C)

    def grad_rims(x, carry):
        grims[0, x] = grad[x, E - 2 :].reshape(2 * E, C).astype(BF16)
        grims[1, x] = grad[x, :2].reshape(2 * E, C).astype(BF16)
        return carry

    lax.fori_loop(0, E, grad_rims, 0)
    send(grims.at[0], ghalos.at[0], halo_send.at[2], halo_recv.at[2], above)
    send(grims.at[1], ghalos.at[1], halo_send.at[3], halo_recv.at[3], below)


    kernel_rows[...] = jnp.zeros_like(kernel_rows)

    def kernel_layer(tap_z):
        for group in ((0, 1), (2, 3), (4,)):
            sums = {}
            for z in range(E):
                factor = grad[:, z]
                own = 2 <= z + tap_z < 2 + E
                for tap_y in group:
                    window = padded[tap_y, :, z + tap_z]
                    for tap_x in range(K):
                        low, high = (max(0, 2 - tap_x), min(E, E + 2 - tap_x)) if own else (0, E)
                        part = window[low + tap_x : high + tap_x] * factor[low:high]
                        part = jnp.sum(part, axis=0)
                        tap = (tap_y, tap_x)
                        sums[tap] = sums[tap] + part if tap in sums else part
            for (tap_y, tap_x), total in sums.items():
                row = (tap_z * K + tap_y) * K + tap_x
                kernel_rows[row : row + 1, 0:C] = jnp.sum(total, axis=0, keepdims=True)

    for tap_z in range(K):
        kernel_layer(tap_z)
    k_out1[...] = kernel_rows[...].astype(BF16).reshape(K_TILES, TILE, LANES)
    send_all(
        x_peers, lambda peer: k_out1.at[pl.ds(peer * K_SHARE, K_SHARE)],
        lambda slot: k_in1.at[slot], send_sem.at[5], recv_sem.at[5],
    )

    wait_bytes(w_in1, recv_sem.at[0])
    total = add_all(w_out1[pl.ds(sample * W_SHARE, W_SHARE)], w_in1, NS - 1)
    w_out2[0:W_SHARE] = total.astype(BF16)
    if NY * PART > W_SHARE:
        w_out2[W_SHARE : NY * PART] = jnp.zeros((NY * PART - W_SHARE, TILE, LANES), BF16)
    send_all(
        y_peers, lambda peer: w_out2.at[pl.ds(peer * PART, PART)],
        lambda slot: w_in2.at[slot], send_sem.at[1], recv_sem.at[1],
    )

    def own_grad_column(x, carry):
        spread_own(gpadded, x, grad[x], y_index)
        return carry

    lax.fori_loop(0, E, own_grad_column, 0)

    conv_own(gpadded, weights, conv, True)

    wait_bytes(k_in1, recv_sem.at[5])
    total = add_all(k_out1[pl.ds(sample * K_SHARE, K_SHARE)], k_in1, NS - 1)
    k_out2[...] = total.astype(BF16)
    send_all(
        y_peers, lambda peer: k_out2, lambda slot: k_in2.at[slot], send_sem.at[6], recv_sem.at[6]
    )

    wait_bytes(w_in2, recv_sem.at[1])
    total = add_all(w_out2[pl.ds(chip_y * PART, PART)], w_in2, NY - 1)
    w_out3[...] = total.astype(BF16)
    hear(2)
    send_all(
        z_peers, lambda peer: w_out3, lambda slot: w_in3.at[slot], send_sem.at[2], recv_sem.at[2]
    )

    for side in range(2):
        wait_bytes(ghalos.at[side], halo_recv.at[2 + side])
    place_halos(gpadded, ghalos)

    wait_bytes(k_in2, recv_sem.at[6])
    k_out3[...] = add_all(k_out2[...], k_in2, NY - 1).astype(BF16)
    send_all(
        z_peers, lambda peer: k_out3, lambda slot: k_in3.at[slot], send_sem.at[7], recv_sem.at[7]
    )

    conv_halo(gpadded, weights, conv, True)

    for x in range(E):
        lanes = slice(x * C, (x + 1) * C)
        mixed_ref[:, :, lanes] = mixed[x].astype(BF16)
        gfield_ref[:, :, lanes] = (upstream[x] + conv[x] * fluid[x]).astype(BF16)
    stores[0].start()
    stores[1].start()

    wait_bytes(w_in3, recv_sem.at[2])
    mine = pl.ds(chip_y * PART, PART)
    w_share[mine] = add_all(w_out3[...], w_in3, NZ - 1).astype(BF16)
    send_all(
        y_peers, lambda peer: w_share.at[mine], lambda slot: w_share.at[mine],
        send_sem.at[3], recv_sem.at[3],
    )

    wait_bytes(k_in3, recv_sem.at[7])
    k_share[...] = add_all(k_out3[...], k_in3, NZ - 1).astype(BF16)
    k_mine = k_hbm.at[pl.ds(sample * K_SHARE, K_SHARE)]
    send_all(
        x_peers, lambda peer: k_share, lambda slot: k_mine, send_sem.at[8], recv_sem.at[8]
    )
    k_keep = pltpu.make_async_copy(k_share, k_mine, store_sem.at[2])
    k_keep.start()

    wait_bytes(w_share.at[0 : (NY - 1) * PART], recv_sem.at[3])
    mine = w_hbm.at[pl.ds(sample * W_SHARE, W_SHARE)]
    send_all(
        x_peers, lambda peer: w_share.at[0:W_SHARE], lambda slot: mine,
        send_sem.at[4], recv_sem.at[4],
    )
    keep = pltpu.make_async_copy(w_share.at[0:W_SHARE], mine, store_sem.at[3])
    keep.start()

    for side in range(2):
        wait_bytes(rims.at[side], halo_send.at[side])
        wait_bytes(grims.at[side], halo_send.at[2 + side])
    sent = (
        w_in1, w_in2, w_in3, w_share.at[0 : (NY - 1) * PART], w_hbm.at[0 : (NS - 1) * W_SHARE],
        k_in1, k_in2, k_in3, k_hbm.at[0 : (NS - 1) * K_SHARE],
    )
    for index, ref in enumerate(sent):
        wait_bytes(ref, send_sem.at[index])
    for store in stores:
        store.wait()
    keep.wait()
    k_keep.wait()
    wait_bytes(k_hbm.at[0 : (NS - 1) * K_SHARE], recv_sem.at[8])
    wait_bytes(w_hbm.at[0 : (NS - 1) * W_SHARE], recv_sem.at[4])


def write_out(
    mixed_in, gfield_in, k_in, w_in,
    mixed_out, gfield_out, gkernel_out, gwin_out, gwout_out, gbin_out, gvec_out,
    mixed, gfield, gkernel, gwin, gwout, gbin, gvec, k_tiles, w_tiles, sem,
):
    def copies(pairs, first):
        return [pltpu.make_async_copy(a, b, sem.at[first + i]) for i, (a, b) in enumerate(pairs)]

    loads = copies([(w_in, w_tiles), (k_in, k_tiles), (mixed_in, mixed), (gfield_in, gfield)], 0)
    stores = copies([
        (mixed, mixed_out), (gfield, gfield_out), (gkernel, gkernel_out), (gwin, gwin_out),
        (gwout, gwout_out), (gbin, gbin_out), (gvec, gvec_out),
    ], 4)
    for load in loads:
        load.start()
    loads[0].wait()
    for base, dest in ((0, gwin), (18, gwout)):
        for part in range(H // LANES):
            block = w_tiles[base + 6 * part : base + 6 * part + 6].astype(F32) * PARAM_SCALE
            dest[:, part * LANES : (part + 1) * LANES] = block.reshape(C, LANES)
    last = w_tiles[36].astype(F32) * PARAM_SCALE
    gbin[...] = last[0:3]
    gvec[...] = last[3:7, 0:C]
    for store in stores[3:]:
        store.start()
    loads[1].wait()
    rows = k_tiles[...].astype(F32).reshape(K_TILES * TILE, LANES)[:, 0:C] * PARAM_SCALE
    for pair in range(K * K):
        gkernel[pair // K, pair % K] = rows[pair * K : (pair + 1) * K]
    stores[2].start()
    for load, store in zip(loads[2:], stores):
        load.wait()
        store.start()
    for store in stores:
        store.wait()


def local(
    features, wall_mask, block_positions, dw_kernel, norm_gain, norm_bias, w_in, b_in, w_out, b_out,
    layer_scale, upstream,
):
    voxels = (E, E, E, C)
    spread = (K, E + 4, E + 4, E, C)
    rows = E**3
    hbm = pl.BlockSpec(memory_space=pltpu.HBM)
    outs = (
        jax.ShapeDtypeStruct((E, E, E * C), BF16),
        jax.ShapeDtypeStruct((E, E, E * C), BF16),
        jax.ShapeDtypeStruct((K, K, K, C), F32),
        jax.ShapeDtypeStruct((C, H), F32),
        jax.ShapeDtypeStruct((C, H), F32),
        jax.ShapeDtypeStruct((H // LANES, LANES), F32),
        jax.ShapeDtypeStruct((4, C), F32),
    )
    scratch = [
        pltpu.VMEM((K * K, K, E, C), F32),
        pltpu.VMEM(spread, F32),
        pltpu.VMEM(spread, F32),
        pltpu.VMEM(voxels, F32),
        pltpu.VMEM(voxels, F32),
        pltpu.VMEM(voxels, F32),
        pltpu.VMEM(voxels, F32),
        pltpu.VMEM(voxels, F32),
        pltpu.VMEM(voxels, F32),
        pltpu.VMEM((rows, C), BF16),
        pltpu.VMEM((rows, H), BF16),
        pltpu.VMEM((rows, H), BF16),
        pltpu.VMEM((rows, C), BF16),
        pltpu.VMEM((4, E, C), F32),
        pltpu.VMEM((E, H), F32),
        pltpu.VMEM((K_TILES * TILE, LANES), F32),
        pltpu.VMEM((TILE, LANES), F32),
        pltpu.VMEM((2, E, 2 * E, C), BF16),
        pltpu.VMEM((2, E, 2 * E, C), BF16),
        pltpu.VMEM((2, E, 2 * E, C), BF16),
        pltpu.VMEM((2, E, 2 * E, C), BF16),
        *(pltpu.VMEM((*lead, TILE, LANES), BF16) for lead in (
            (W_TILES,), (NS - 1, W_SHARE), (NY * PART,), (NY - 1, PART), (PART,), (NZ - 1, PART),
            (NY * PART,),
            (K_TILES,), (NS - 1, K_SHARE), (K_SHARE,), (NY - 1, K_SHARE), (K_SHARE,),
            (NZ - 1, K_SHARE), (K_SHARE,),
        )),
        *(pltpu.VMEM(shape, dtype) for shape, dtype in (
            ((E, E, E * C), BF16), ((E, E * E), jnp.int32), ((1, NY * NZ), jnp.int32),
            ((K, K, K, C), F32), ((1, C), F32), ((1, C), F32), ((C, H), BF16),
            ((H // LANES, LANES), F32), ((C, H), BF16), ((1, C), F32), ((1, C), F32),
            ((E, E, E * C), BF16),
        )),
        *(pltpu.VMEM(out.shape, out.dtype) for out in outs[:2]),
        pltpu.SemaphoreType.DMA((4,)),
        pltpu.SemaphoreType.DMA((4,)),
        pltpu.SemaphoreType.DMA((9,)),
        pltpu.SemaphoreType.DMA((9,)),
        pltpu.SemaphoreType.DMA((12,)),
        pltpu.SemaphoreType.DMA((4,)),
        pltpu.SemaphoreType.REGULAR((3,)),
    ]
    results = pl.pallas_call(
        body,
        out_shape=outs[:2] + tuple(
            jax.ShapeDtypeStruct((tiles, TILE, LANES), BF16) for tiles in (K_TILES, W_TILES)
        ),
        in_specs=[hbm] * 12,
        out_specs=[hbm] * 4,
        scratch_shapes=scratch,
        compiler_params=pltpu.CompilerParams(
            collective_id=0, has_side_effects=True, vmem_limit_bytes=VMEM_BYTES
        ),
        cost_estimate=pl.CostEstimate(flops=400_000_000, bytes_accessed=1_500_000, transcendentals=200_000),
        name="block_step",
    )(
        features[0, 0, 0],
        wall_mask[0, 0, 0],
        block_positions[:, :, 0],
        dw_kernel,
        norm_gain[None],
        norm_bias[None],
        w_in,
        b_in.reshape(H // LANES, LANES),
        w_out.T,
        b_out[None],
        layer_scale[None],
        upstream[0, 0, 0],
    )
    results = pl.pallas_call(
        write_out,
        out_shape=outs,
        in_specs=[hbm] * 4,
        out_specs=[hbm] * 7,
        scratch_shapes=[
            *(pltpu.VMEM(out.shape, out.dtype) for out in outs),
            pltpu.VMEM((K_TILES, TILE, LANES), BF16),
            pltpu.VMEM((W_TILES, TILE, LANES), BF16),
            pltpu.SemaphoreType.DMA((11,)),
        ],
        compiler_params=pltpu.CompilerParams(vmem_limit_bytes=VMEM_BYTES),
        cost_estimate=pl.CostEstimate(flops=0, bytes_accessed=1_000_000, transcendentals=0),
        name="write_results",
    )(*results)
    mixed, gfield, gkernel, gwin, gwout, gbin, gvec = results
    return (mixed[None, None, None], gfield[None, None, None], gkernel, gwin, gwout.T, gbin.reshape(H), gvec)


def solution(mesh):
    sharded = P("sample", "space", None, None, None, None)
    return jax.shard_map(
        local,
        mesh=mesh,
        in_specs=(
            sharded,
            P("sample", "space", None, None, None),
            P("sample", None, None),
            P(), P(), P(), P(), P(), P(), P(), P(),
            sharded,
        ),
        out_specs=(sharded, sharded, P(), P(), P(), P(), P()),
        check_vma=False,
    )
```
